128 devices in a mesh: blk: 16 (over z, x), grid: 8 (over y, core).
Axes of the slice: x: 4, y: 4, z: 4, core: 2. Of those that a mesh axis runs over, the one named last changes fastest.
Arguments:
- state: bfloat16 [256, 2048, 128], P('grid', 'blk'), may hold values from -6 to 6
- courant: float32 [256, 2048], P('grid', 'blk'), may hold values from 0.2 to 0.5
- diffusion: float32 [128], replicated, may hold values from 0.02 to 0.12
- table_value: bfloat16 [4096, 128], P('blk'), may hold values from -6 to 6
- table_base: bfloat16 [4096, 128], P('blk'), may hold values from -6 to 6
- table_sens: bfloat16 [4096, 128, 128], P('blk'), may hold values from -0.5 to 0.5
- slot_cell: int32 [8, 768, 128], P('grid', 'blk'), may hold values from -1 to 4095, as said below
- hit_step: int32 [8, 768, 128], P('grid', 'blk'), may hold values from 0 to 15, as said below
- entry_ids: int32 [16, 8, 768], P('blk', 'grid'), may hold values from 0 to 255
Outputs:
- advanced: float32 [256, 2048, 128], P('grid', 'blk')
The draws below stay inside these ranges and needn't reach their ends.
Inputs may be any that keep to these rules, and one draw needn't show every extreme that they name: `slot_cell`: on each device, its 48 blocks of 128 slots hold each of its 4096 local cells in exactly one slot; all other slots hold -1. `hit_step`: on each device, at most 512 occupied slots name any one partition, and in every draw some partition is named by exactly 512 of them on each device.
All inputs are finite; a program needn't handle non-finite values.
Results may differ from the reference program's by a relative error of at most 0.0038.
Values may be sent and summed in bfloat16 or wider, within the bound.
No kernel may reach another device: no remote copies, remote signals or barrier semaphores. Data moves between devices by JAX's collectives and lax.ppermute only.
A program may use at most 192 MiB of HBM per device.

```python
import math
import jax
import jax.numpy as jnp
from jax import lax

S = 128
QB = 128
CX = 32
CY = 128
E_DEV = 256
NB = 48
NX = 256
NY = 2048
ENTRIES = 4096
BLOCKS = 768
N_BLK = 16
N_GRID = 8


def slot_layout(key):
    key = jax.random.fold_in(key, 7)
    keys = jax.random.split(key, N_GRID * N_BLK)

    def single(subkey):
        order = jax.random.permutation(subkey, NB * QB)
        return jnp.where(order < CX * CY, order, -1).astype(jnp.int32).reshape(NB, QB)
    return jax.vmap(single)(keys)


def draw_slot_cell(key, part):
    return slot_layout(key).reshape(N_GRID, N_BLK * NB, QB)


def draw_hit_step(key, part):
    layout = slot_layout(key)
    key = jax.random.fold_in(key, 11)
    cells = CX * CY
    most = max(2, 2 * cells // N_BLK)
    keys = jax.random.split(key, N_GRID * N_BLK)
    blk_of = jnp.arange(N_GRID * N_BLK, dtype=jnp.int32) % N_BLK

    def single(subkey, slots, blk):
        first, second, third = jax.random.split(subkey, 3)
        hottest = jax.random.randint(first, (), 0, N_BLK)
        places = jnp.arange(cells, dtype=jnp.int32)
        offset = jnp.where(places < most, 0, 1 + (places - most) % (N_BLK - 1))
        dest_of_place = (hottest + offset) % N_BLK
        dest_of_cell = dest_of_place[jax.random.permutation(second, cells)]
        filler = jax.random.randint(third, slots.shape, 0, N_BLK)
        dest = jnp.where(slots >= 0, dest_of_cell[jnp.maximum(slots, 0)], filler)
        return ((dest - blk) % N_BLK).astype(jnp.int32)
    result = jax.vmap(single)(keys, layout, blk_of)
    return result.reshape(N_GRID, N_BLK * NB, QB)


def with_ends(values, key, low, high):
    spot = [jax.random.randint(jax.random.fold_in(key, axis), (), 0, length) for axis, length in enumerate(values.shape)]
    main_axis = values.shape.index(max(values.shape))
    next_to = spot[:main_axis] + [(spot[main_axis] + 1) % values.shape[main_axis]] + spot[main_axis + 1:]
    return values.at[tuple(spot)].set(low).at[tuple(next_to)].set(high)


def level_of(stream_key, dims, cuts, low, high):
    def one(axis_at, parts):
        heights = jax.random.uniform(jax.random.fold_in(jax.random.fold_in(stream_key, 6), axis_at), (parts,), jnp.float32, low / len(cuts), high / len(cuts))
        return jnp.repeat(jnp.exp(heights), dims[axis_at] // parts).reshape((-1,) + (1,) * (len(dims) - axis_at - 1))

    factor_of = one(*cuts[0])
    for cut in cuts[1:]:
        factor_of = factor_of * one(*cut)
    return factor_of


def normal_values(stream_key, extent, spread, limit, cuts=(), kind=jnp.bfloat16):
    level = level_of(stream_key, extent, cuts, -0.22, 0.18) if cuts else 1.0
    drawn = jax.random.normal(stream_key, extent, jnp.float32) * spread * level
    return jnp.minimum(jnp.maximum(drawn, -limit), limit).astype(kind)


def setup_inputs(seed: int = 0) -> dict:
    key_of = jax.random.split(jax.random.key(seed), 10)
    state = normal_values(key_of[0], (NX, NY, S), 1.0, 6.0, ((0, 8), (1, 16)))
    courant = jnp.clip(0.2 + 0.3 * jax.random.uniform(key_of[1], (NX, NY), jnp.float32) ** level_of(key_of[1], (NX, NY), ((0, 8), (1, 16)), -0.2, 0.2), 0.2, 0.5)
    diffusion = jnp.clip(jnp.exp(jax.random.uniform(key_of[2], (S,), jnp.float32, math.log(0.02), math.log(0.12))), 0.02, 0.12)
    table_value = normal_values(key_of[3], (ENTRIES, S), 1.0, 6.0, ((0, 16),))
    table_base = normal_values(key_of[4], (ENTRIES, S), 1.0, 6.0, ((0, 16),))
    table_sens = normal_values(key_of[5], (ENTRIES, S, S), S ** -0.5, 0.5, ((0, 16),))
    slot_cell = draw_slot_cell(jax.random.fold_in(key_of[9], 71), 0)
    hit_step = draw_hit_step(jax.random.fold_in(key_of[9], 71), 0)
    entry_ids = with_ends(jax.random.randint(key_of[8], (N_BLK, N_GRID, BLOCKS), 0, E_DEV), jax.random.fold_in(key_of[8], 1), 0, E_DEV - 1).astype(jnp.int32)
    return {"state": state, "courant": courant, "diffusion": diffusion, "table_value": table_value, "table_base": table_base, "table_sens": table_sens, "slot_cell": slot_cell, "hit_step": hit_step, "entry_ids": entry_ids}


def reference(state, courant, diffusion, table_value, table_base, table_sens, slot_cell, hit_step, entry_ids):
    slots = slot_cell.reshape(N_GRID, N_BLK, NB, QB)
    hits = hit_step.reshape(N_GRID, N_BLK, NB, QB)
    entries = entry_ids.reshape(N_BLK, N_GRID, N_BLK, NB)
    grid_ix = jnp.arange(N_GRID, dtype=jnp.int32)[:, None, None, None]
    blk_ix = jnp.arange(N_BLK, dtype=jnp.int32)[None, :, None, None]
    block_ix = jnp.arange(NB, dtype=jnp.int32)[None, None, :, None]
    live = slots >= 0
    cell = jnp.maximum(slots, 0)
    rows = jnp.where(live, grid_ix * CX + cell // CY, NX).astype(jnp.int32)
    cols = (blk_ix * CY + cell % CY + 0 * grid_ix).astype(jnp.int32)
    owner = (blk_ix + hits) % N_BLK
    chosen = entries[owner, grid_ix + 0 * owner, blk_ix + 0 * owner, block_ix + 0 * owner]
    global_entry = (owner * E_DEV + chosen).astype(jnp.int32)
    picked = state[jnp.minimum(rows, NX - 1), cols]
    queries = jnp.where(live[..., None], picked, jnp.zeros_like(picked))
    flat_q = queries.reshape(-1, QB, S)
    flat_e = global_entry.reshape(-1, QB)

    def react_rows(args):
        block, index = args
        base = table_base[index].astype(jnp.float32)
        delta = (block.astype(jnp.float32) - base).astype(jnp.bfloat16)
        sens = table_sens[index].astype(jnp.float32)
        mapped = table_value[index].astype(jnp.float32) + jnp.einsum('qi,qij->qj', delta.astype(jnp.float32), sens)
        return mapped.astype(jnp.bfloat16)

    results = lax.map(react_rows, (flat_q, flat_e))
    reacted = state.at[rows.reshape(-1), cols.reshape(-1)].set(results.reshape(-1, S), mode="drop")
    field = reacted.astype(jnp.float32)
    padded = jnp.pad(field, ((1, 1), (1, 1), (0, 0)))
    upper = padded[:-2, 1:-1]
    lower = padded[2:, 1:-1]
    left_side = padded[1:-1, :-2]
    right_side = padded[1:-1, 2:]
    return field - courant[..., None] * (field - upper) + diffusion * (upper + lower + left_side + right_side - 4.0 * field)
```

```python
import jax
import jax.numpy as jnp
from jax import lax
from jax.experimental import pallas as pl
from jax.experimental.pallas import tpu as pltpu
from jax.sharding import PartitionSpec as P

F32 = jnp.float32
BF16 = jnp.bfloat16
CAP = 512
META = 16
SEG = CAP + META
WIN = 16


def iota(shape, dim):
    return lax.broadcasted_iota(jnp.int32, shape, dim)


def zero_one(mask):
    return jnp.where(mask, 1.0, 0.0).astype(BF16)


def dot(a, b):
    return lax.dot_general(a, b, (((1,), (0,)), ((), ())), preferred_element_type=F32)


def dot_nt(a, b):
    return lax.dot_general(a, b, (((1,), (1,)), ((), ())), preferred_element_type=F32)


def pack_kernel(
    nparts, me_ref, slots_ref, hits_ref, state_ref, send_ref, back_ref,
    field, packed, code_vmem, code_smem, sem,
):
    nblocks, width = slots_ref.shape
    cells = state_ref.shape[0]
    slots = slots_ref[...]
    live = slots >= 0
    cell = jnp.maximum(slots, 0)
    owner = jnp.where(live, (hits_ref[...] + me_ref[0]) & (nparts - 1), nparts)
    before = zero_one(iota((width, width), 0) < iota((width, width), 1))
    both = jnp.concatenate([before, jnp.ones((width, width), BF16)], axis=1)
    earlier = zero_one(iota((nblocks, nblocks), 1) < iota((nblocks, nblocks), 0))
    starts = zero_one(iota((nblocks, width), 0) < iota((nblocks, width), 1))
    ones = jnp.ones((META, width), BF16)
    top = iota((META, width), 0) == 0
    place = jnp.zeros((nblocks, width), F32)
    for part in range(nparts):
        mine = owner == part
        mask = zero_one(mine)
        ranks = dot(mask, both)
        offsets = dot(earlier, ranks[:, width:].astype(BF16))
        place = place + jnp.where(mine, ranks[:, :width] + offsets, 0.0)
        in_lanes = dot_nt(ones, mask).astype(BF16)
        begin = dot(in_lanes, starts)
        high = jnp.floor(begin * (1.0 / 16.0))
        send_ref[pl.ds(part * SEG + CAP, META), :] = jnp.where(
            top, high, begin - 16.0 * high
        ).astype(BF16)
    place = place.astype(jnp.int32)
    forth = jnp.where(live, owner * SEG + place, nparts * SEG)
    code_vmem[...] = forth * cells + cell
    back_ref[...] = jnp.where(live, (owner * CAP + place) * (2 * cells) + cell, cells)
    copy = pltpu.make_async_copy(code_vmem, code_smem, sem)
    copy.start()
    field[...] = state_ref[...].astype(F32)
    copy.wait()

    def block(k, _):
        for q in range(width):
            code = code_smem[k, q]
            packed[pl.ds(code // cells, 1), :] = field[pl.ds(code & (cells - 1), 1), :]
        return 0

    lax.fori_loop(0, nblocks, block, 0)

    def convert(part, _):
        at = pl.multiple_of(part * SEG, 16)
        send_ref[pl.ds(at, CAP), :] = packed[pl.ds(at, CAP), :].astype(BF16)
        return 0

    lax.fori_loop(0, nparts, convert, 0)


def pack(me, slots, hits, flat, nparts):
    nblocks, width = slots.shape
    cells = flat.shape[0]
    return pl.pallas_call(
        lambda *refs: pack_kernel(nparts, *refs),
        out_shape=(
            jax.ShapeDtypeStruct((nparts * SEG, width), BF16),
            jax.ShapeDtypeStruct((nblocks, width), jnp.int32),
        ),
        in_specs=[pl.BlockSpec(memory_space=pltpu.SMEM)]
        + [pl.BlockSpec(memory_space=pltpu.VMEM)] * 3,
        out_specs=[pl.BlockSpec(memory_space=pltpu.VMEM)] * 2,
        scratch_shapes=[
            pltpu.VMEM((cells, width), F32),
            pltpu.VMEM((nparts * SEG + 8, width), F32),
            pltpu.VMEM((nblocks, width), jnp.int32),
            pltpu.SMEM((nblocks, width), jnp.int32),
            pltpu.SemaphoreType.DMA,
        ],
        compiler_params=pltpu.CompilerParams(vmem_limit_bytes=32 << 20),
    )(me, slots, hits, flat)


def react_kernel(
    nparts, nblocks, entries_ref, recv_ref, value_ref, base_ref, sens_ref, out_ref,
    rows, mapped, begin_vmem, begin_smem, sem,
):
    width = recv_ref.shape[1]
    for part in range(nparts):
        meta = recv_ref[pl.ds(part * SEG + CAP, META), :].astype(F32)
        begin_vmem[pl.ds(part, 1), :] = (meta[0:1] * 16.0 + meta[1:2]).astype(jnp.int32)
    copy = pltpu.make_async_copy(begin_vmem, begin_smem, sem)
    copy.start()

    def widen(part, _):
        at = pl.multiple_of(part * SEG, 16)
        rows[pl.ds(at, SEG), :] = recv_ref[pl.ds(at, SEG), :].astype(F32)
        return 0

    lax.fori_loop(0, nparts, widen, 0)
    copy.wait()
    zero = jnp.zeros((WIN, width), BF16)
    four = 4

    def delta(at, entry):
        base = base_ref[pl.ds(entry, 1), :]
        return (rows[pl.ds(at, WIN), :] - base).astype(BF16)

    def fours(step, _):
        part = step // (nblocks // four)
        first = (step % (nblocks // four)) * four
        begins = [begin_smem[part, first + i] for i in range(four + 1)]
        entry = [entries_ref[part * nblocks + first + i] for i in range(four)]
        at = [part * SEG + begins[i] for i in range(four)]
        dx = [delta(at[i], entry[i]) for i in range(four)]
        lhs = jnp.concatenate(
            [
                jnp.concatenate([dx[0], zero], axis=1),
                jnp.concatenate([dx[1], zero], axis=1),
                jnp.concatenate([zero, dx[2]], axis=1),
                jnp.concatenate([zero, dx[3]], axis=1),
            ],
            axis=0,
        )
        rhs = jnp.concatenate(
            [
                jnp.concatenate([sens_ref[entry[0]], sens_ref[entry[1]]], axis=1),
                jnp.concatenate([sens_ref[entry[2]], sens_ref[entry[3]]], axis=1),
            ],
            axis=0,
        )
        product = dot(lhs, rhs)
        for i in range(four):
            half = (i % 2) * width
            mapped[pl.ds(at[i], WIN), :] = (
                product[i * WIN : (i + 1) * WIN, half : half + width]
                + value_ref[pl.ds(entry[i], 1), :]
            )
        counts = [begins[i + 1] - begins[i] for i in range(four)]
        most = jnp.maximum(
            jnp.maximum(counts[0], counts[1]), jnp.maximum(counts[2], counts[3])
        )

        @pl.when(most > WIN)
        def _():
            for i in range(four):

                def more(w, _, i=i):
                    here = at[i] + w * WIN
                    left = counts[i] - w * WIN
                    result = dot(delta(here, entry[i]), sens_ref[entry[i]])
                    result = result + value_ref[pl.ds(entry[i], 1), :]
                    keep = iota((WIN, width), 0) < left
                    mapped[pl.ds(here, WIN), :] = jnp.where(
                        keep, result, mapped[pl.ds(here, WIN), :]
                    )
                    return 0

                lax.fori_loop(1, (counts[i] + WIN - 1) // WIN, more, 0)

        return 0

    lax.fori_loop(0, nparts * nblocks // four, fours, 0)

    def narrow(part, _):
        out_ref[pl.ds(pl.multiple_of(part * CAP, 16), CAP), :] = mapped[
            pl.ds(pl.multiple_of(part * SEG, 16), CAP), :
        ].astype(BF16)
        return 0

    lax.fori_loop(0, nparts, narrow, 0)


def react(entries, recv, value, base, sens, nparts):
    width = recv.shape[1]
    nblocks = entries.shape[0] // nparts
    return pl.pallas_call(
        lambda *refs: react_kernel(nparts, nblocks, *refs),
        out_shape=jax.ShapeDtypeStruct((nparts * CAP, width), BF16),
        in_specs=[pl.BlockSpec(memory_space=pltpu.SMEM)]
        + [pl.BlockSpec(memory_space=pltpu.VMEM)] * 4,
        out_specs=pl.BlockSpec(memory_space=pltpu.VMEM),
        scratch_shapes=[
            pltpu.VMEM((nparts * SEG, width), F32),
            pltpu.VMEM((nparts * SEG, width), F32),
            pltpu.VMEM((nparts, width), jnp.int32),
            pltpu.SMEM((nparts, width), jnp.int32),
            pltpu.SemaphoreType.DMA,
        ],
        compiler_params=pltpu.CompilerParams(vmem_limit_bytes=48 << 20),
    )(entries, recv, value.astype(F32), base.astype(F32), sens)


def unpack_kernel(code_ref, ret_ref, out_ref, rows, field):
    nblocks, width = code_ref.shape
    cells = out_ref.shape[0]
    rows[...] = ret_ref[...].astype(F32)

    def block(k, _):
        for q in range(width):
            code = code_ref[k, q]
            field[pl.ds(code & (2 * cells - 1), 1), :] = rows[
                pl.ds(code // (2 * cells), 1), :
            ]
        return 0

    lax.fori_loop(0, nblocks, block, 0)
    out_ref[...] = field[pl.ds(0, cells), :].astype(BF16)


def unpack(code, ret, cells):
    width = ret.shape[1]
    return pl.pallas_call(
        unpack_kernel,
        out_shape=jax.ShapeDtypeStruct((cells, width), BF16),
        in_specs=[
            pl.BlockSpec(memory_space=pltpu.SMEM),
            pl.BlockSpec(memory_space=pltpu.VMEM),
        ],
        out_specs=pl.BlockSpec(memory_space=pltpu.VMEM),
        scratch_shapes=[
            pltpu.VMEM(ret.shape, F32),
            pltpu.VMEM((cells + 8, width), F32),
        ],
        compiler_params=pltpu.CompilerParams(vmem_limit_bytes=32 << 20),
    )(code, ret)


def transport_kernel(
    mid_ref, up_ref, down_ref, left_ref, right_ref, courant_ref, diffusion_ref, out_ref
):
    rows_here, cols, width = mid_ref.shape
    diffusion = diffusion_ref[...]
    first = iota((cols, width), 0) == 0
    last = iota((cols, width), 0) == cols - 1

    def row(i):
        if i < 0:
            return up_ref[...].astype(F32)
        if i >= rows_here:
            return down_ref[...].astype(F32)
        return mid_ref[i].astype(F32)

    above, here = row(-1), row(0)
    for i in range(rows_here):
        below = row(i + 1)
        left = jnp.where(first, left_ref[i : i + 1, :].astype(F32), pltpu.roll(here, 1, 0))
        right = jnp.where(
            last, right_ref[i : i + 1, :].astype(F32), pltpu.roll(here, cols - 1, 0)
        )
        courant = courant_ref[:, i : i + 1]
        out_ref[i] = (
            here
            - courant * (here - above)
            + diffusion * (above + below + left + right - 4.0 * here)
        )
        above, here = here, below


def transport(reacted, up, down, left, right, courant, diffusion):
    shape = reacted.shape
    return pl.pallas_call(
        transport_kernel,
        out_shape=jax.ShapeDtypeStruct(shape, F32),
        in_specs=[pl.BlockSpec(memory_space=pltpu.VMEM)] * 7,
        out_specs=pl.BlockSpec(memory_space=pltpu.VMEM),
        compiler_params=pltpu.CompilerParams(vmem_limit_bytes=32 << 20),
    )(reacted, up, down, left, right, courant, diffusion)


def shifted(block, axis, ahead):
    count = lax.axis_size(axis)
    forward = [(i, i + 1) for i in range(count - 1)]
    return lax.ppermute(block, axis, forward if ahead else [(j, i) for i, j in forward])


def local(
    state, courant, diffusion, table_value, table_base, table_sens, slot_cell, hit_step, entry_ids
):
    rows_here, cols_here, width = state.shape
    cells = rows_here * cols_here
    nparts = lax.axis_size("blk")
    me = lax.axis_index("blk").astype(jnp.int32).reshape(1)
    flat = state.reshape(cells, width)
    send, code = pack(me, slot_cell[0], hit_step[0], flat, nparts)
    recv = lax.all_to_all(send.reshape(nparts, SEG, width), "blk", 0, 0, tiled=True)
    done = react(
        entry_ids[0, 0], recv.reshape(nparts * SEG, width),
        table_value, table_base, table_sens, nparts,
    )
    back = lax.all_to_all(done.reshape(nparts, CAP, width), "blk", 0, 0, tiled=True)
    reacted = unpack(code, back.reshape(nparts * CAP, width), cells)
    reacted = reacted.reshape(rows_here, cols_here, width)
    left = shifted(reacted[:, -1], "blk", True)
    right = shifted(reacted[:, 0], "blk", False)
    up = shifted(reacted[-1], "grid", True)
    down = shifted(reacted[0], "grid", False)
    return transport(
        reacted, up, down, left, right, courant.T, diffusion.reshape(1, width)
    )


def solution(mesh):
    return jax.shard_map(
        local,
        mesh=mesh,
        in_specs=(
            P("grid", "blk", None),
            P("grid", "blk"),
            P(),
            P("blk", None),
            P("blk", None),
            P("blk", None, None),
            P("grid", "blk", None),
            P("grid", "blk", None),
            P("blk", "grid", None),
        ),
        out_specs=P("grid", "blk", None),
        check_vma=False,
    )
```

```python
import jax
import jax.numpy as jnp
from jax import lax
from jax.experimental import pallas as pl
from jax.experimental.pallas import tpu as pltpu
from jax.sharding import PartitionSpec as P

F32 = jnp.float32
BF16 = jnp.bfloat16
CAP = 512
META = 16
SEG = CAP + META
WIN = 16
GROUPS = 48
GROUP = 16


def iota(shape, dim):
    return lax.broadcasted_iota(jnp.int32, shape, dim)


def zero_one(mask):
    return jnp.where(mask, 1.0, 0.0).astype(BF16)


def dot(a, b):
    return lax.dot_general(a, b, (((1,), (0,)), ((), ())), preferred_element_type=F32)


def dot_nt(a, b):
    return lax.dot_general(a, b, (((1,), (1,)), ((), ())), preferred_element_type=F32)


def pack_kernel(
    nparts, me_ref, slots_hbm, hits_hbm, state_hbm, send_hbm, back_ref,
    slots_ref, hits_ref, state_ref, field, packed, send_ref, code_vmem, code_smem, sems, out_sems,
):
    nblocks, width = slots_ref.shape
    cells = state_ref.shape[0]
    rows_here = cells // width
    loads = [
        pltpu.make_async_copy(slots_hbm, slots_ref, sems.at[0]),
        pltpu.make_async_copy(hits_hbm, hits_ref, sems.at[1]),
        pltpu.make_async_copy(state_hbm, state_ref, sems.at[2]),
    ]
    for load in loads:
        load.start()
    before = zero_one(iota((width, width), 0) < iota((width, width), 1))
    both = jnp.concatenate([before, jnp.ones((width, width), BF16)], axis=1)
    earlier = zero_one(iota((nblocks, nblocks), 1) < iota((nblocks, nblocks), 0))
    starts = zero_one(iota((nblocks, width), 0) < iota((nblocks, width), 1))
    ones = jnp.ones((META, width), BF16)
    top = iota((META, width), 0) == 0
    loads[0].wait()
    loads[1].wait()
    slots = slots_ref[...]
    live = slots >= 0
    owner = jnp.where(live, (hits_ref[...] + me_ref[0]) & (nparts - 1), nparts)
    place = jnp.zeros((nblocks, width), F32)
    for part in range(nparts):
        mine = owner == part
        mask = zero_one(mine)
        ranks = dot(mask, both)
        offsets = dot(earlier, ranks[:, width:].astype(BF16))
        place = place + jnp.where(mine, ranks[:, :width] + offsets, 0.0)
        in_lanes = dot_nt(ones, mask).astype(BF16)
        begin = dot(in_lanes, starts)
        high = jnp.floor(begin * (1.0 / 16.0))
        send_ref[pl.ds(part * SEG + CAP, META), :] = jnp.where(
            top, high, begin - 16.0 * high
        ).astype(BF16)
    spot = owner * CAP + place.astype(jnp.int32)
    spot_high = (spot >> 7).astype(F32)
    spot_low = (spot & 127).astype(F32)
    cell_row = slots >> 7
    cell_col = slots & 127
    total = jnp.zeros((2 * rows_here, width), F32)
    row_ids = iota((rows_here, width), 0)
    col_ids = iota((width, width), 0)
    for pair in range(0, nblocks, 2):
        lhs, rhs = [], []
        for k in (pair, pair + 1):
            at_row = row_ids == cell_row[k : k + 1, :]
            lhs.append(
                jnp.concatenate(
                    [
                        jnp.where(at_row, spot_high[k : k + 1, :], 0.0),
                        jnp.where(at_row, spot_low[k : k + 1, :], 0.0),
                    ],
                    axis=0,
                ).astype(BF16)
            )
            rhs.append(zero_one(col_ids == cell_col[k : k + 1, :]))
        total = total + dot_nt(jnp.concatenate(lhs, axis=1), jnp.concatenate(rhs, axis=1))
    back = (total[:rows_here] * 128.0 + total[rows_here:]).astype(jnp.int32)
    back_ref[...] = back
    code_vmem[...] = back + (back >> 9) * META
    copy = pltpu.make_async_copy(code_vmem, code_smem, sems.at[3])
    copy.start()
    loads[2].wait()
    field[...] = state_ref[...].astype(F32)
    copy.wait()

    def line(i, _):
        for q in range(0, width, GROUP):
            values = [field[pl.ds(i * width + q + j, 1), :] for j in range(GROUP)]
            spots = [code_smem[i, q + j] for j in range(GROUP)]
            for value, at in zip(values, spots):
                packed[pl.ds(at, 1), :] = value
        return 0

    lax.fori_loop(0, rows_here, line, 0)
    stores = []
    for part in range(nparts):
        send_ref[pl.ds(part * SEG, CAP), :] = packed[pl.ds(part * SEG, CAP), :].astype(BF16)
        stores.append(
            pltpu.make_async_copy(
                send_ref.at[pl.ds(part * SEG, SEG), :],
                send_hbm.at[pl.ds(part * SEG, SEG), :],
                out_sems.at[part],
            )
        )
        stores[-1].start()
    for store in stores:
        store.wait()


def pack(me, slots, hits, flat, nparts):
    nblocks, width = slots.shape
    cells = flat.shape[0]
    return pl.pallas_call(
        lambda *refs: pack_kernel(nparts, *refs),
        out_shape=(
            jax.ShapeDtypeStruct((nparts * SEG, width), BF16),
            jax.ShapeDtypeStruct((cells // width, width), jnp.int32),
        ),
        in_specs=[pl.BlockSpec(memory_space=pltpu.SMEM)]
        + [pl.BlockSpec(memory_space=pltpu.HBM)] * 3,
        out_specs=[pl.BlockSpec(memory_space=pltpu.HBM), pl.BlockSpec(memory_space=pltpu.VMEM)],
        scratch_shapes=[
            pltpu.VMEM((nblocks, width), jnp.int32),
            pltpu.VMEM((nblocks, width), jnp.int32),
            pltpu.VMEM((cells, width), BF16),
            pltpu.VMEM((cells, width), F32),
            pltpu.VMEM((nparts * SEG, width), F32),
            pltpu.VMEM((nparts * SEG, width), BF16),
            pltpu.VMEM((cells // width, width), jnp.int32),
            pltpu.SMEM((cells // width, width), jnp.int32),
            pltpu.SemaphoreType.DMA((4,)),
            pltpu.SemaphoreType.DMA((nparts,)),
        ],
        compiler_params=pltpu.CompilerParams(vmem_limit_bytes=62 << 20),
    )(me, slots, hits, flat)


def react_kernel(
    nparts, nblocks, entries_ref, recv_ref, value_ref, base_ref, sens_ref, out_ref,
    rows, mapped, values, bases, begin_vmem, begin_smem, sem,
):
    width = recv_ref.shape[1]
    values[...] = value_ref[...].astype(F32)
    bases[...] = base_ref[...].astype(F32)
    for part in range(nparts):
        meta = recv_ref[pl.ds(part * SEG + CAP, META), :].astype(F32)
        begin_vmem[pl.ds(part, 1), :] = (meta[0:1] * 16.0 + meta[1:2]).astype(jnp.int32)
    copy = pltpu.make_async_copy(begin_vmem, begin_smem, sem)
    copy.start()

    def widen(part, _):
        at = pl.multiple_of(part * SEG, 16)
        rows[pl.ds(at, SEG), :] = recv_ref[pl.ds(at, SEG), :].astype(F32)
        return 0

    lax.fori_loop(0, nparts, widen, 0)
    copy.wait()
    zero = jnp.zeros((WIN, width), BF16)
    four = 4

    def delta(at, entry):
        base = bases[pl.ds(entry, 1), :]
        return (rows[pl.ds(at, WIN), :] - base).astype(BF16)

    def batch(part, first):
        begins = [begin_smem[part, first + i] for i in range(GROUPS + 1)]
        entry = [entries_ref[0, 0, part * nblocks + first + i] for i in range(GROUPS)]
        at = [part * SEG + begins[i] for i in range(GROUPS)]
        dx = [delta(at[i], entry[i]) for i in range(GROUPS)]
        results = []
        for i in range(0, GROUPS, four):
            lhs = jnp.concatenate(
                [
                    jnp.concatenate([dx[i], zero], axis=1),
                    jnp.concatenate([dx[i + 1], zero], axis=1),
                    jnp.concatenate([zero, dx[i + 2]], axis=1),
                    jnp.concatenate([zero, dx[i + 3]], axis=1),
                ],
                axis=0,
            )
            rhs = jnp.concatenate(
                [
                    jnp.concatenate([sens_ref[entry[i]], sens_ref[entry[i + 1]]], axis=1),
                    jnp.concatenate([sens_ref[entry[i + 2]], sens_ref[entry[i + 3]]], axis=1),
                ],
                axis=0,
            )
            product = dot(lhs, rhs)
            for j in range(four):
                half = (j % 2) * width
                results.append(
                    product[j * WIN : (j + 1) * WIN, half : half + width]
                    + values[pl.ds(entry[i + j], 1), :]
                )
        for i in range(GROUPS):
            mapped[pl.ds(at[i], WIN), :] = results[i]
        counts = [begins[i + 1] - begins[i] for i in range(GROUPS)]
        most = counts[0]
        for count in counts[1:]:
            most = jnp.maximum(most, count)

        @pl.when(most > WIN)
        def _():
            for i in range(GROUPS):

                def more(w, _, i=i):
                    here = at[i] + w * WIN
                    left = counts[i] - w * WIN
                    result = dot(delta(here, entry[i]), sens_ref[entry[i]])
                    result = result + values[pl.ds(entry[i], 1), :]
                    keep = iota((WIN, width), 0) < left
                    mapped[pl.ds(here, WIN), :] = jnp.where(
                        keep, result, mapped[pl.ds(here, WIN), :]
                    )
                    return 0

                lax.fori_loop(1, (counts[i] + (WIN - 1)) >> 4, more, 0)

    def source(part, _):
        def batches(step, _):
            batch(part, step * GROUPS)
            return 0

        return lax.fori_loop(0, nblocks // GROUPS, batches, 0)

    lax.fori_loop(0, nparts, source, 0)

    def narrow(part, _):
        out_ref[pl.ds(pl.multiple_of(part * CAP, 16), CAP), :] = mapped[
            pl.ds(pl.multiple_of(part * SEG, 16), CAP), :
        ].astype(BF16)
        return 0

    lax.fori_loop(0, nparts, narrow, 0)


def react(entries, recv, value, base, sens, nparts):
    width = recv.shape[1]
    nblocks = entries.shape[-1] // nparts
    return pl.pallas_call(
        lambda *refs: react_kernel(nparts, nblocks, *refs),
        out_shape=jax.ShapeDtypeStruct((nparts * CAP, width), BF16),
        in_specs=[pl.BlockSpec(memory_space=pltpu.SMEM)]
        + [pl.BlockSpec(memory_space=pltpu.VMEM)] * 4,
        out_specs=pl.BlockSpec(memory_space=pltpu.VMEM),
        scratch_shapes=[
            pltpu.VMEM((nparts * SEG, width), F32),
            pltpu.VMEM((nparts * SEG, width), F32),
            pltpu.VMEM(value.shape, F32),
            pltpu.VMEM(base.shape, F32),
            pltpu.VMEM((nparts, width), jnp.int32),
            pltpu.SMEM((nparts, width), jnp.int32),
            pltpu.SemaphoreType.DMA,
        ],
        compiler_params=pltpu.CompilerParams(vmem_limit_bytes=24 << 20),
    )(entries, recv, value, base, sens)


def unpack_kernel(code_ref, ret_ref, out_ref, rows):
    rows_here, width = code_ref.shape
    rows[...] = ret_ref[...].astype(F32)

    def line(i, _):
        for q in range(0, width, GROUP):
            spots = [code_ref[i, q + j] for j in range(GROUP)]
            values = [rows[pl.ds(at, 1), :] for at in spots]
            out_ref[pl.ds(pl.multiple_of(i * width + q, GROUP), GROUP), :] = jnp.concatenate(
                values, axis=0
            ).astype(BF16)
        return 0

    lax.fori_loop(0, rows_here, line, 0)


def unpack(code, ret, cells):
    width = ret.shape[1]
    return pl.pallas_call(
        unpack_kernel,
        out_shape=jax.ShapeDtypeStruct((cells, width), BF16),
        in_specs=[
            pl.BlockSpec(memory_space=pltpu.SMEM),
            pl.BlockSpec(memory_space=pltpu.VMEM),
        ],
        out_specs=pl.BlockSpec(memory_space=pltpu.VMEM),
        scratch_shapes=[pltpu.VMEM(ret.shape, F32)],
        compiler_params=pltpu.CompilerParams(vmem_limit_bytes=20 << 20),
    )(code, ret)


def transport_kernel(
    mid_ref, up_ref, down_ref, left_ref, right_ref, courant_ref, diffusion_ref, out_ref
):
    rows_here, cols, width = mid_ref.shape
    diffusion = diffusion_ref[...]
    first = iota((cols, width), 0) == 0
    last = iota((cols, width), 0) == cols - 1

    def row(i):
        if i < 0:
            return up_ref[...].astype(F32)
        if i >= rows_here:
            return down_ref[...].astype(F32)
        return mid_ref[i].astype(F32)

    above, here = row(-1), row(0)
    for i in range(rows_here):
        below = row(i + 1)
        left = jnp.where(first, left_ref[i : i + 1, :].astype(F32), pltpu.roll(here, 1, 0))
        right = jnp.where(
            last, right_ref[i : i + 1, :].astype(F32), pltpu.roll(here, cols - 1, 0)
        )
        courant = courant_ref[:, i : i + 1]
        out_ref[i] = (
            here
            - courant * (here - above)
            + diffusion * (above + below + left + right - 4.0 * here)
        )
        above, here = here, below


def transport(reacted, up, down, left, right, courant, diffusion):
    shape = reacted.shape
    return pl.pallas_call(
        transport_kernel,
        out_shape=jax.ShapeDtypeStruct(shape, F32),
        in_specs=[pl.BlockSpec(memory_space=pltpu.VMEM)] * 7,
        out_specs=pl.BlockSpec(memory_space=pltpu.VMEM),
        compiler_params=pltpu.CompilerParams(vmem_limit_bytes=20 << 20),
    )(reacted, up, down, left, right, courant, diffusion)


def shifted(block, axis, ahead):
    count = lax.axis_size(axis)
    forward = [(i, i + 1) for i in range(count - 1)]
    return lax.ppermute(block, axis, forward if ahead else [(j, i) for i, j in forward])


def local(
    state, courant, diffusion, table_value, table_base, table_sens, slot_cell, hit_step, entry_ids
):
    rows_here, cols_here, width = state.shape
    cells = rows_here * cols_here
    nparts = lax.axis_size("blk")
    me = lax.axis_index("blk").astype(jnp.int32).reshape(1)
    flat = state.reshape(cells, width)
    send, code = pack(me, slot_cell[0], hit_step[0], flat, nparts)
    recv = lax.all_to_all(send.reshape(nparts, SEG, width), "blk", 0, 0, tiled=True)
    done = react(
        entry_ids, recv.reshape(nparts * SEG, width),
        table_value, table_base, table_sens, nparts,
    )
    back = lax.all_to_all(done.reshape(nparts, CAP, width), "blk", 0, 0, tiled=True)
    reacted = unpack(code, back.reshape(nparts * CAP, width), cells)
    reacted = reacted.reshape(rows_here, cols_here, width)
    left = shifted(reacted[:, -1], "blk", True)
    right = shifted(reacted[:, 0], "blk", False)
    up = shifted(reacted[-1], "grid", True)
    down = shifted(reacted[0], "grid", False)
    return transport(
        reacted, up, down, left, right, courant.T, diffusion.reshape(1, width)
    )


def solution(mesh):
    return jax.shard_map(
        local,
        mesh=mesh,
        in_specs=(
            P("grid", "blk", None),
            P("grid", "blk"),
            P(),
            P("blk", None),
            P("blk", None),
            P("blk", None, None),
            P("grid", "blk", None),
            P("grid", "blk", None),
            P("blk", "grid", None),
        ),
        out_specs=P("grid", "blk", None),
        check_vma=False,
    )
```

```python
import jax
import jax.numpy as jnp
from jax import lax
from jax.experimental import pallas as pl
from jax.experimental.pallas import tpu as pltpu
from jax.sharding import PartitionSpec as P

F32 = jnp.float32
BF16 = jnp.bfloat16
CAP = 512
META = 16
SEG = CAP + META
WIN = 16
GROUPS = 48
LINES = 4
GROUP = 16


def iota(shape, dim):
    return lax.broadcasted_iota(jnp.int32, shape, dim)


def zero_one(mask):
    return jnp.where(mask, 1.0, 0.0).astype(BF16)


def dot(a, b):
    return lax.dot_general(a, b, (((1,), (0,)), ((), ())), preferred_element_type=F32)


def dot_nt(a, b):
    return lax.dot_general(a, b, (((1,), (1,)), ((), ())), preferred_element_type=F32)


def pack_kernel(
    nparts, me_ref, slots_hbm, hits_hbm, state_hbm, send_hbm, back_ref,
    slots_ref, hits_ref, state_ref, field, packed, send_ref, code_vmem, code_smem, sems, out_sems,
):
    nblocks, width = slots_ref.shape
    cells = state_ref.shape[0]
    rows_here = cells // width
    loads = [
        pltpu.make_async_copy(slots_hbm, slots_ref, sems.at[0]),
        pltpu.make_async_copy(hits_hbm, hits_ref, sems.at[1]),
        pltpu.make_async_copy(state_hbm, state_ref, sems.at[2]),
    ]
    for load in loads:
        load.start()
    before = zero_one(iota((width, width), 0) < iota((width, width), 1))
    weights = jnp.concatenate([jnp.ones((width, width), BF16), before], axis=0)
    earlier = zero_one(iota((width, nblocks), 1) < iota((width, nblocks), 0))
    ones = jnp.ones((META, width), BF16)
    top = iota((META, width), 0) == 0
    loads[0].wait()
    loads[1].wait()
    slots = slots_ref[...]
    live = slots >= 0
    owner = jnp.where(live, (hits_ref[...] + me_ref[0]) & (nparts - 1), nparts)
    mine = [owner == part for part in range(nparts)]
    masks = [zero_one(each) for each in mine]
    ahead = [dot(earlier, mask).astype(BF16) for mask in masks]
    ranks = dot(
        jnp.concatenate(
            [jnp.concatenate([a[:nblocks], m], axis=1) for a, m in zip(ahead, masks)], axis=0
        ),
        weights,
    )
    begins = dot_nt(ones, jnp.concatenate(ahead, axis=0))
    place = jnp.zeros((nblocks, width), F32)
    for part in range(nparts):
        place = place + jnp.where(mine[part], ranks[part * nblocks : (part + 1) * nblocks], 0.0)
        begin = begins[:, part * width : (part + 1) * width]
        high = jnp.floor(begin * (1.0 / 16.0))
        send_ref[pl.ds(part * SEG + CAP, META), :] = jnp.where(
            top, high, begin - 16.0 * high
        ).astype(BF16)
    spot = owner * CAP + place.astype(jnp.int32)
    spot_high = (spot >> 7).astype(F32)
    spot_low = (spot & 127).astype(F32)
    cell_row = slots >> 7
    cell_col = slots & 127
    total = jnp.zeros((2 * rows_here, width), F32)
    row_ids = iota((rows_here, width), 0)
    col_ids = iota((width, width), 0)
    for pair in range(0, nblocks, 2):
        lhs, rhs = [], []
        for k in (pair, pair + 1):
            at_row = row_ids == cell_row[k : k + 1, :]
            lhs.append(
                jnp.concatenate(
                    [
                        jnp.where(at_row, spot_high[k : k + 1, :], 0.0),
                        jnp.where(at_row, spot_low[k : k + 1, :], 0.0),
                    ],
                    axis=0,
                ).astype(BF16)
            )
            rhs.append(zero_one(col_ids == cell_col[k : k + 1, :]))
        total = total + dot_nt(jnp.concatenate(lhs, axis=1), jnp.concatenate(rhs, axis=1))
    back = (total[:rows_here] * 128.0 + total[rows_here:]).astype(jnp.int32)
    back_ref[...] = back
    code_vmem[...] = back + (back >> 9) * META
    copy = pltpu.make_async_copy(code_vmem, code_smem, sems.at[3])
    copy.start()
    loads[2].wait()
    field[...] = state_ref[...].astype(F32)
    copy.wait()

    def line(i, _):
        for q in range(0, width, GROUP):
            values = [field[pl.ds(i * width + q + j, 1), :] for j in range(GROUP)]
            spots = [code_smem[i, q + j] for j in range(GROUP)]
            for value, at in zip(values, spots):
                packed[pl.ds(at, 1), :] = value
        return 0

    lax.fori_loop(0, rows_here, line, 0)
    stores = []
    for part in range(nparts):
        send_ref[pl.ds(part * SEG, CAP), :] = packed[pl.ds(part * SEG, CAP), :].astype(BF16)
        stores.append(
            pltpu.make_async_copy(
                send_ref.at[pl.ds(part * SEG, SEG), :],
                send_hbm.at[pl.ds(part * SEG, SEG), :],
                out_sems.at[part],
            )
        )
        stores[-1].start()
    for store in stores:
        store.wait()


def pack(me, slots, hits, flat, nparts):
    nblocks, width = slots.shape
    cells = flat.shape[0]
    return pl.pallas_call(
        lambda *refs: pack_kernel(nparts, *refs),
        out_shape=(
            jax.ShapeDtypeStruct((nparts * SEG, width), BF16),
            jax.ShapeDtypeStruct((cells // width, width), jnp.int32),
        ),
        in_specs=[pl.BlockSpec(memory_space=pltpu.SMEM)]
        + [pl.BlockSpec(memory_space=pltpu.HBM)] * 3,
        out_specs=[pl.BlockSpec(memory_space=pltpu.HBM), pl.BlockSpec(memory_space=pltpu.VMEM)],
        scratch_shapes=[
            pltpu.VMEM((nblocks, width), jnp.int32),
            pltpu.VMEM((nblocks, width), jnp.int32),
            pltpu.VMEM((cells, width), BF16),
            pltpu.VMEM((cells, width), F32),
            pltpu.VMEM((nparts * SEG, width), F32),
            pltpu.VMEM((nparts * SEG, width), BF16),
            pltpu.VMEM((cells // width, width), jnp.int32),
            pltpu.SMEM((cells // width, width), jnp.int32),
            pltpu.SemaphoreType.DMA((4,)),
            pltpu.SemaphoreType.DMA((nparts,)),
        ],
        compiler_params=pltpu.CompilerParams(vmem_limit_bytes=62 << 20),
    )(me, slots, hits, flat)


def react_kernel(
    nparts, nblocks, entries_ref, recv_ref, value_ref, base_ref, sens_ref, out_ref,
    rows, mapped, values, bases, begin_vmem, begin_smem, sem,
):
    width = recv_ref.shape[1]
    values[...] = value_ref[...].astype(F32)
    bases[...] = base_ref[...].astype(F32)
    for part in range(nparts):
        meta = recv_ref[pl.ds(part * SEG + CAP, META), :].astype(F32)
        begin_vmem[pl.ds(part, 1), :] = (meta[0:1] * 16.0 + meta[1:2]).astype(jnp.int32)
    copy = pltpu.make_async_copy(begin_vmem, begin_smem, sem)
    copy.start()

    def widen(part, _):
        at = pl.multiple_of(part * SEG, 16)
        rows[pl.ds(at, SEG), :] = recv_ref[pl.ds(at, SEG), :].astype(F32)
        return 0

    lax.fori_loop(0, nparts, widen, 0)
    copy.wait()
    zero = jnp.zeros((WIN, width), BF16)
    four = 4

    def delta(at, entry):
        base = bases[pl.ds(entry, 1), :]
        return (rows[pl.ds(at, WIN), :] - base).astype(BF16)

    def batch(part, first):
        begins = [begin_smem[part, first + i] for i in range(GROUPS + 1)]
        entry = [entries_ref[0, 0, part * nblocks + first + i] for i in range(GROUPS)]
        at = [part * SEG + begins[i] for i in range(GROUPS)]
        dx = [delta(at[i], entry[i]) for i in range(GROUPS)]
        results = []
        for i in range(0, GROUPS, four):
            lhs = jnp.concatenate(
                [
                    jnp.concatenate([dx[i], zero], axis=1),
                    jnp.concatenate([dx[i + 1], zero], axis=1),
                    jnp.concatenate([zero, dx[i + 2]], axis=1),
                    jnp.concatenate([zero, dx[i + 3]], axis=1),
                ],
                axis=0,
            )
            rhs = jnp.concatenate(
                [
                    jnp.concatenate([sens_ref[entry[i]], sens_ref[entry[i + 1]]], axis=1),
                    jnp.concatenate([sens_ref[entry[i + 2]], sens_ref[entry[i + 3]]], axis=1),
                ],
                axis=0,
            )
            product = dot(lhs, rhs)
            for j in range(four):
                half = (j % 2) * width
                results.append(
                    product[j * WIN : (j + 1) * WIN, half : half + width]
                    + values[pl.ds(entry[i + j], 1), :]
                )
        for i in range(GROUPS):
            mapped[pl.ds(at[i], WIN), :] = results[i]
        counts = [begins[i + 1] - begins[i] for i in range(GROUPS)]
        most = counts[0]
        for count in counts[1:]:
            most = jnp.maximum(most, count)

        @pl.when(most > WIN)
        def _():
            for i in range(GROUPS):

                def more(w, _, i=i):
                    here = at[i] + w * WIN
                    left = counts[i] - w * WIN
                    result = dot(delta(here, entry[i]), sens_ref[entry[i]])
                    result = result + values[pl.ds(entry[i], 1), :]
                    keep = iota((WIN, width), 0) < left
                    mapped[pl.ds(here, WIN), :] = jnp.where(
                        keep, result, mapped[pl.ds(here, WIN), :]
                    )
                    return 0

                lax.fori_loop(1, (counts[i] + (WIN - 1)) >> 4, more, 0)

    def source(part, _):
        def batches(step, _):
            batch(part, step * GROUPS)
            return 0

        return lax.fori_loop(0, nblocks // GROUPS, batches, 0)

    lax.fori_loop(0, nparts, source, 0)

    def narrow(part, _):
        out_ref[pl.ds(pl.multiple_of(part * CAP, 16), CAP), :] = mapped[
            pl.ds(pl.multiple_of(part * SEG, 16), CAP), :
        ].astype(BF16)
        return 0

    lax.fori_loop(0, nparts, narrow, 0)


def react(entries, recv, value, base, sens, nparts):
    width = recv.shape[1]
    nblocks = entries.shape[-1] // nparts
    return pl.pallas_call(
        lambda *refs: react_kernel(nparts, nblocks, *refs),
        out_shape=jax.ShapeDtypeStruct((nparts * CAP, width), BF16),
        in_specs=[pl.BlockSpec(memory_space=pltpu.SMEM)]
        + [pl.BlockSpec(memory_space=pltpu.VMEM)] * 4,
        out_specs=pl.BlockSpec(memory_space=pltpu.VMEM),
        scratch_shapes=[
            pltpu.VMEM((nparts * SEG, width), F32),
            pltpu.VMEM((nparts * SEG, width), F32),
            pltpu.VMEM(value.shape, F32),
            pltpu.VMEM(base.shape, F32),
            pltpu.VMEM((nparts, width), jnp.int32),
            pltpu.SMEM((nparts, width), jnp.int32),
            pltpu.SemaphoreType.DMA,
        ],
        compiler_params=pltpu.CompilerParams(vmem_limit_bytes=24 << 20),
    )(entries, recv, value, base, sens)


def edges_kernel(code_ref, ret_ref, up_ref, down_ref, left_ref, right_ref, rows):
    rows_here, width = code_ref.shape
    cols_here = width
    rows[...] = ret_ref[...].astype(F32)

    def gather(out, spots):
        for first in range(0, len(spots), GROUP):
            out[pl.ds(first, GROUP), :] = jnp.concatenate(
                [rows[pl.ds(at, 1), :] for at in spots[first : first + GROUP]], axis=0
            ).astype(BF16)

    gather(up_ref, [code_ref[rows_here - 1, j] for j in range(cols_here)])
    gather(down_ref, [code_ref[0, j] for j in range(cols_here)])
    gather(left_ref, [code_ref[i, cols_here - 1] for i in range(rows_here)])
    gather(right_ref, [code_ref[i, 0] for i in range(rows_here)])


def edges(code, ret):
    rows_here, width = code.shape
    ends = [rows_here if side else width for side in (0, 0, 1, 1)]
    return pl.pallas_call(
        edges_kernel,
        out_shape=[jax.ShapeDtypeStruct((end, width), BF16) for end in ends],
        in_specs=[
            pl.BlockSpec(memory_space=pltpu.SMEM),
            pl.BlockSpec(memory_space=pltpu.VMEM),
        ],
        out_specs=[pl.BlockSpec(memory_space=pltpu.VMEM)] * 4,
        scratch_shapes=[pltpu.VMEM(ret.shape, F32)],
        compiler_params=pltpu.CompilerParams(vmem_limit_bytes=20 << 20),
    )(code, ret)


def unpack_kernel(code_ref, ret_ref, out_ref, rows):
    rows_here, width = code_ref.shape
    rows[...] = ret_ref[...].astype(F32)

    def line(i, _):
        for q in range(0, width, GROUP):
            spots = [code_ref[i, q + j] for j in range(GROUP)]
            values = [rows[pl.ds(at, 1), :] for at in spots]
            for j, value in enumerate(values):
                out_ref[pl.ds(i * width + q + j, 1), :] = value
        return 0

    lax.fori_loop(0, rows_here, line, 0)


def unpack(code, ret):
    cells, width = code.size, ret.shape[1]
    return pl.pallas_call(
        unpack_kernel,
        out_shape=jax.ShapeDtypeStruct((cells, width), F32),
        in_specs=[
            pl.BlockSpec(memory_space=pltpu.SMEM),
            pl.BlockSpec(memory_space=pltpu.VMEM),
        ],
        out_specs=pl.BlockSpec(memory_space=pltpu.VMEM),
        scratch_shapes=[pltpu.VMEM(ret.shape, F32)],
        compiler_params=pltpu.CompilerParams(vmem_limit_bytes=20 << 20),
        cost_estimate=pl.CostEstimate(flops=0, bytes_accessed=16 << 20, transcendentals=0),
    )(code, ret)


def transport_kernel(
    mid_ref, up_ref, down_ref, left_ref, right_ref, courant_ref, diffusion_ref, out_hbm,
    out_ref, sems,
):
    rows_here, cols, width = mid_ref.shape
    diffusion = diffusion_ref[...]
    first = iota((cols, width), 0) == 0
    last = iota((cols, width), 0) == cols - 1

    def row(i):
        if i < 0:
            return up_ref[...].astype(F32)
        if i >= rows_here:
            return down_ref[...].astype(F32)
        return mid_ref[i]

    stores = []
    above, here = row(-1), row(0)
    for i in range(rows_here):
        below = row(i + 1)
        left = jnp.where(first, left_ref[i : i + 1, :].astype(F32), pltpu.roll(here, 1, 0))
        right = jnp.where(
            last, right_ref[i : i + 1, :].astype(F32), pltpu.roll(here, cols - 1, 0)
        )
        courant = courant_ref[:, i : i + 1]
        out_ref[i] = (
            here
            - courant * (here - above)
            + diffusion * (above + below + left + right - 4.0 * here)
        )
        above, here = here, below
        if i % LINES == LINES - 1:
            piece = pl.ds(i + 1 - LINES, LINES)
            stores.append(
                pltpu.make_async_copy(out_ref.at[piece], out_hbm.at[piece], sems.at[i // LINES])
            )
            stores[-1].start()
    for store in stores:
        store.wait()


def transport(reacted, up, down, left, right, courant, diffusion):
    shape = reacted.shape
    return pl.pallas_call(
        transport_kernel,
        out_shape=jax.ShapeDtypeStruct(shape, F32),
        in_specs=[pl.BlockSpec(memory_space=pltpu.VMEM)] * 7,
        out_specs=pl.BlockSpec(memory_space=pl.ANY),
        scratch_shapes=[
            pltpu.VMEM(shape, F32),
            pltpu.SemaphoreType.DMA((shape[0] // LINES,)),
        ],
        compiler_params=pltpu.CompilerParams(vmem_limit_bytes=20 << 20),
    )(reacted, up, down, left, right, courant, diffusion)


def shifted(block, axis, ahead):
    count = lax.axis_size(axis)
    forward = [(i, i + 1) for i in range(count - 1)]
    return lax.ppermute(block, axis, forward if ahead else [(j, i) for i, j in forward])


def local(
    state, courant, diffusion, table_value, table_base, table_sens, slot_cell, hit_step, entry_ids
):
    rows_here, cols_here, width = state.shape
    cells = rows_here * cols_here
    nparts = lax.axis_size("blk")
    me = lax.axis_index("blk").astype(jnp.int32).reshape(1)
    flat = state.reshape(cells, width)
    send, code = pack(me, slot_cell[0], hit_step[0], flat, nparts)
    recv = lax.all_to_all(send.reshape(nparts, SEG, width), "blk", 0, 0, tiled=True)
    done = react(
        entry_ids, recv.reshape(nparts * SEG, width),
        table_value, table_base, table_sens, nparts,
    )
    back = lax.all_to_all(done.reshape(nparts, CAP, width), "blk", 0, 0, tiled=True)
    back = back.reshape(nparts * CAP, width)
    last_line, first_line, last_column, first_column = edges(code, back)
    up = shifted(last_line, "grid", True)
    down = shifted(first_line, "grid", False)
    left = shifted(last_column, "blk", True)
    right = shifted(first_column, "blk", False)
    reacted = unpack(code, back).reshape(rows_here, cols_here, width)
    return transport(
        reacted, up, down, left, right, courant.T, diffusion.reshape(1, width)
    )


def solution(mesh):
    return jax.shard_map(
        local,
        mesh=mesh,
        in_specs=(
            P("grid", "blk", None),
            P("grid", "blk"),
            P(),
            P("blk", None),
            P("blk", None),
            P("blk", None, None),
            P("grid", "blk", None),
            P("grid", "blk", None),
            P("blk", "grid", None),
        ),
        out_specs=P("grid", "blk", None),
        check_vma=False,
    )
```

```python
import jax
import jax.numpy as jnp
from jax import lax
from jax.experimental import pallas as pl
from jax.experimental.pallas import tpu as pltpu
from jax.sharding import PartitionSpec as P

F32 = jnp.float32
BF16 = jnp.bfloat16
CAP = 512
META = 16
SEG = CAP + META
WIN = 16
GROUPS = 48
LINES = 4
PARTS = 4
GROUP = 16


def iota(shape, dim):
    return lax.broadcasted_iota(jnp.int32, shape, dim)


def zero_one(mask):
    return jnp.where(mask, 1.0, 0.0).astype(BF16)


def dot(a, b):
    return lax.dot_general(a, b, (((1,), (0,)), ((), ())), preferred_element_type=F32)


def dot_nt(a, b):
    return lax.dot_general(a, b, (((1,), (1,)), ((), ())), preferred_element_type=F32)


def pack_kernel(
    nparts, me_ref, slots_hbm, hits_hbm, state_hbm, sens_hbm, send_ref, back_ref, sens_ref,
    slots_ref, hits_ref, state_ref, field, packed, code_vmem, code_smem, sems,
):
    nblocks, width = slots_ref.shape
    cells = state_ref.shape[0]
    rows_here = cells // width
    loads = [
        pltpu.make_async_copy(slots_hbm, slots_ref, sems.at[0]),
        pltpu.make_async_copy(hits_hbm, hits_ref, sems.at[1]),
        pltpu.make_async_copy(state_hbm, state_ref, sems.at[2]),
    ]
    for load in loads:
        load.start()
    fetch = pltpu.make_async_copy(sens_hbm, sens_ref, sems.at[4])
    fetch.start()
    before = zero_one(iota((width, width), 0) < iota((width, width), 1))
    weights = jnp.concatenate([jnp.ones((width, width), BF16), before], axis=0)
    earlier = zero_one(iota((width, nblocks), 1) < iota((width, nblocks), 0))
    ones = jnp.ones((META, width), BF16)
    top = iota((META, width), 0) == 0
    loads[0].wait()
    loads[1].wait()
    slots = slots_ref[...]
    live = slots >= 0
    owner = jnp.where(live, (hits_ref[...] + me_ref[0]) & (nparts - 1), nparts)
    mine = [owner == part for part in range(nparts)]
    masks = [zero_one(each) for each in mine]
    ahead = [dot(earlier, mask).astype(BF16) for mask in masks]
    ranks = dot(
        jnp.concatenate(
            [jnp.concatenate([a[:nblocks], m], axis=1) for a, m in zip(ahead, masks)], axis=0
        ),
        weights,
    )
    begins = dot_nt(ones, jnp.concatenate(ahead, axis=0))
    place = jnp.zeros((nblocks, width), F32)
    for part in range(nparts):
        place = place + jnp.where(mine[part], ranks[part * nblocks : (part + 1) * nblocks], 0.0)
        begin = begins[:, part * width : (part + 1) * width]
        high = jnp.floor(begin * (1.0 / 16.0))
        send_ref[pl.ds(part * SEG + CAP, META), :] = jnp.where(
            top, high, begin - 16.0 * high
        ).astype(BF16)
    spot = owner * CAP + place.astype(jnp.int32)
    spot_high = (spot >> 7).astype(F32)
    spot_low = (spot & 127).astype(F32)
    cell_row = slots >> 7
    cell_col = slots & 127
    total = jnp.zeros((2 * rows_here, width), F32)
    row_ids = iota((rows_here, width), 0)
    col_ids = iota((width, width), 0)
    for pair in range(0, nblocks, 2):
        lhs, rhs = [], []
        for k in (pair, pair + 1):
            at_row = row_ids == cell_row[k : k + 1, :]
            lhs.append(
                jnp.concatenate(
                    [
                        jnp.where(at_row, spot_high[k : k + 1, :], 0.0),
                        jnp.where(at_row, spot_low[k : k + 1, :], 0.0),
                    ],
                    axis=0,
                ).astype(BF16)
            )
            rhs.append(zero_one(col_ids == cell_col[k : k + 1, :]))
        total = total + dot_nt(jnp.concatenate(lhs, axis=1), jnp.concatenate(rhs, axis=1))
    back = (total[:rows_here] * 128.0 + total[rows_here:]).astype(jnp.int32)
    back_ref[...] = back
    code_vmem[...] = back + (back >> 9) * META
    copy = pltpu.make_async_copy(code_vmem, code_smem, sems.at[3])
    copy.start()
    loads[2].wait()
    field[...] = state_ref[...].astype(F32)
    copy.wait()

    def line(i, _):
        for q in range(0, width, GROUP):
            values = [field[pl.ds(i * width + q + j, 1), :] for j in range(GROUP)]
            spots = [code_smem[i, q + j] for j in range(GROUP)]
            for value, at in zip(values, spots):
                packed[pl.ds(at, 1), :] = value
        return 0

    lax.fori_loop(0, rows_here, line, 0)
    for part in range(nparts):
        send_ref[pl.ds(part * SEG, CAP), :] = packed[pl.ds(part * SEG, CAP), :].astype(BF16)
    fetch.wait()


def pack(me, slots, hits, flat, sens, nparts):
    nblocks, width = slots.shape
    cells = flat.shape[0]
    return pl.pallas_call(
        lambda *refs: pack_kernel(nparts, *refs),
        out_shape=(
            jax.ShapeDtypeStruct((nparts * SEG, width), BF16),
            jax.ShapeDtypeStruct((cells // width, width), jnp.int32),
            pltpu.VMEM(sens.shape, BF16),
        ),
        in_specs=[pl.BlockSpec(memory_space=pltpu.SMEM)]
        + [pl.BlockSpec(memory_space=pltpu.HBM)] * 4,
        out_specs=[pl.BlockSpec(memory_space=pltpu.VMEM)] * 3,
        scratch_shapes=[
            pltpu.VMEM((nblocks, width), jnp.int32),
            pltpu.VMEM((nblocks, width), jnp.int32),
            pltpu.VMEM((cells, width), BF16),
            pltpu.VMEM((cells, width), F32),
            pltpu.VMEM((nparts * SEG, width), F32),
            pltpu.VMEM((cells // width, width), jnp.int32),
            pltpu.SMEM((cells // width, width), jnp.int32),
            pltpu.SemaphoreType.DMA((5,)),
        ],
        compiler_params=pltpu.CompilerParams(vmem_limit_bytes=36 << 20),
    )(me, *[pltpu.with_memory_space_constraint(each, pltpu.HBM) for each in (slots, hits, flat, sens)])


def react_kernel(
    nparts, nblocks, entries_ref, recv_ref, value_ref, base_ref, sens_ref, out_ref,
    rows, mapped, values, bases, begin_vmem, begin_smem, sem,
):
    width = recv_ref.shape[1]
    values[...] = value_ref[...].astype(F32)
    bases[...] = base_ref[...].astype(F32)
    for part in range(nparts):
        meta = recv_ref[pl.ds(part * SEG + CAP, META), :].astype(F32)
        begin_vmem[pl.ds(part, 1), :] = (meta[0:1] * 16.0 + meta[1:2]).astype(jnp.int32)
    copy = pltpu.make_async_copy(begin_vmem, begin_smem, sem)
    copy.start()

    def widen(part, _):
        at = pl.multiple_of(part * SEG, 16)
        rows[pl.ds(at, SEG), :] = recv_ref[pl.ds(at, SEG), :].astype(F32)
        return 0

    lax.fori_loop(0, nparts, widen, 0)
    copy.wait()
    zero = jnp.zeros((WIN, width), BF16)
    four = 4

    def delta(at, entry):
        base = bases[pl.ds(entry, 1), :]
        return (rows[pl.ds(at, WIN), :] - base).astype(BF16)

    def batch(part, first):
        begins = [begin_smem[part, first + i] for i in range(GROUPS + 1)]
        entry = [entries_ref[0, 0, part * nblocks + first + i] for i in range(GROUPS)]
        at = [part * SEG + begins[i] for i in range(GROUPS)]
        dx = [delta(at[i], entry[i]) for i in range(GROUPS)]
        results = []
        for i in range(0, GROUPS, four):
            lhs = jnp.concatenate(
                [
                    jnp.concatenate([dx[i], zero], axis=1),
                    jnp.concatenate([dx[i + 1], zero], axis=1),
                    jnp.concatenate([zero, dx[i + 2]], axis=1),
                    jnp.concatenate([zero, dx[i + 3]], axis=1),
                ],
                axis=0,
            )
            rhs = jnp.concatenate(
                [
                    jnp.concatenate([sens_ref[entry[i]], sens_ref[entry[i + 1]]], axis=1),
                    jnp.concatenate([sens_ref[entry[i + 2]], sens_ref[entry[i + 3]]], axis=1),
                ],
                axis=0,
            )
            product = dot(lhs, rhs)
            for j in range(four):
                half = (j % 2) * width
                results.append(
                    product[j * WIN : (j + 1) * WIN, half : half + width]
                    + values[pl.ds(entry[i + j], 1), :]
                )
        for i in range(GROUPS):
            mapped[pl.ds(at[i], WIN), :] = results[i]
        counts = [begins[i + 1] - begins[i] for i in range(GROUPS)]
        most = counts[0]
        for count in counts[1:]:
            most = jnp.maximum(most, count)

        def rest():
            for i in range(GROUPS):

                def more(w, _, i=i):
                    here = at[i] + w * WIN
                    left = counts[i] - w * WIN
                    result = dot(delta(here, entry[i]), sens_ref[entry[i]])
                    result = result + values[pl.ds(entry[i], 1), :]
                    keep = iota((WIN, width), 0) < left
                    mapped[pl.ds(here, WIN), :] = jnp.where(
                        keep, result, mapped[pl.ds(here, WIN), :]
                    )
                    return 0

                lax.fori_loop(1, (counts[i] + (WIN - 1)) >> 4, more, 0)

        return most > WIN, rest

    def sources(step, _):
        rests = [batch(step * PARTS + i, 0) for i in range(PARTS)]
        for needed, rest in rests:
            pl.when(needed)(rest)
        return 0

    lax.fori_loop(0, nparts // PARTS, sources, 0)

    def narrow(part, _):
        out_ref[pl.ds(pl.multiple_of(part * CAP, 16), CAP), :] = mapped[
            pl.ds(pl.multiple_of(part * SEG, 16), CAP), :
        ].astype(BF16)
        return 0

    lax.fori_loop(0, nparts, narrow, 0)


def react(entries, recv, value, base, sens, nparts):
    width = recv.shape[1]
    nblocks = entries.shape[-1] // nparts
    return pl.pallas_call(
        lambda *refs: react_kernel(nparts, nblocks, *refs),
        out_shape=jax.ShapeDtypeStruct((nparts * CAP, width), BF16),
        in_specs=[pl.BlockSpec(memory_space=pltpu.SMEM)]
        + [pl.BlockSpec(memory_space=pltpu.VMEM)] * 4,
        out_specs=pl.BlockSpec(memory_space=pltpu.VMEM),
        scratch_shapes=[
            pltpu.VMEM((nparts * SEG, width), F32),
            pltpu.VMEM((nparts * SEG, width), F32),
            pltpu.VMEM(value.shape, F32),
            pltpu.VMEM(base.shape, F32),
            pltpu.VMEM((nparts, width), jnp.int32),
            pltpu.SMEM((nparts, width), jnp.int32),
            pltpu.SemaphoreType.DMA,
        ],
        compiler_params=pltpu.CompilerParams(vmem_limit_bytes=24 << 20),
    )(entries, recv, value, base, sens)


def edges_kernel(code_ref, ret_ref, up_ref, down_ref, left_ref, right_ref, rows):
    rows_here, width = code_ref.shape
    cols_here = width
    rows[...] = ret_ref[...].astype(F32)

    def gather(out, spots):
        for first in range(0, len(spots), GROUP):
            out[pl.ds(first, GROUP), :] = jnp.concatenate(
                [rows[pl.ds(at, 1), :] for at in spots[first : first + GROUP]], axis=0
            ).astype(BF16)

    gather(up_ref, [code_ref[rows_here - 1, j] for j in range(cols_here)])
    gather(down_ref, [code_ref[0, j] for j in range(cols_here)])
    gather(left_ref, [code_ref[i, cols_here - 1] for i in range(rows_here)])
    gather(right_ref, [code_ref[i, 0] for i in range(rows_here)])


def edges(code, ret):
    rows_here, width = code.shape
    ends = [rows_here if side else width for side in (0, 0, 1, 1)]
    return pl.pallas_call(
        edges_kernel,
        out_shape=[jax.ShapeDtypeStruct((end, width), BF16) for end in ends],
        in_specs=[
            pl.BlockSpec(memory_space=pltpu.SMEM),
            pl.BlockSpec(memory_space=pltpu.VMEM),
        ],
        out_specs=[pl.BlockSpec(memory_space=pltpu.VMEM)] * 4,
        scratch_shapes=[pltpu.VMEM(ret.shape, F32)],
        compiler_params=pltpu.CompilerParams(vmem_limit_bytes=20 << 20),
    )(code, ret)


def unpack_kernel(code_ref, ret_ref, out_ref, rows):
    rows_here, width = code_ref.shape
    rows[...] = ret_ref[...].astype(F32)

    def line(i, _):
        for q in range(0, width, GROUP):
            spots = [code_ref[i, q + j] for j in range(GROUP)]
            values = [rows[pl.ds(at, 1), :] for at in spots]
            for j, value in enumerate(values):
                out_ref[pl.ds(i * width + q + j, 1), :] = value
        return 0

    lax.fori_loop(0, rows_here, line, 0)


def unpack(code, ret):
    cells, width = code.size, ret.shape[1]
    return pl.pallas_call(
        unpack_kernel,
        out_shape=jax.ShapeDtypeStruct((cells, width), F32),
        in_specs=[
            pl.BlockSpec(memory_space=pltpu.SMEM),
            pl.BlockSpec(memory_space=pltpu.VMEM),
        ],
        out_specs=pl.BlockSpec(memory_space=pltpu.VMEM),
        scratch_shapes=[pltpu.VMEM(ret.shape, F32)],
        compiler_params=pltpu.CompilerParams(vmem_limit_bytes=20 << 20),
        cost_estimate=pl.CostEstimate(flops=0, bytes_accessed=16 << 20, transcendentals=0),
    )(code, ret)


def transport_kernel(
    mid_ref, up_ref, down_ref, left_ref, right_ref, courant_ref, diffusion_ref, out_hbm,
    out_ref, sems,
):
    rows_here, cols, width = mid_ref.shape
    diffusion = diffusion_ref[...]
    first = iota((cols, width), 0) == 0
    last = iota((cols, width), 0) == cols - 1

    def row(i):
        if i < 0:
            return up_ref[...].astype(F32)
        if i >= rows_here:
            return down_ref[...].astype(F32)
        return mid_ref[i]

    stores = []
    above, here = row(-1), row(0)
    for i in range(rows_here):
        below = row(i + 1)
        left = jnp.where(first, left_ref[i : i + 1, :].astype(F32), pltpu.roll(here, 1, 0))
        right = jnp.where(
            last, right_ref[i : i + 1, :].astype(F32), pltpu.roll(here, cols - 1, 0)
        )
        courant = courant_ref[:, i : i + 1]
        out_ref[i] = (
            here
            - courant * (here - above)
            + diffusion * (above + below + left + right - 4.0 * here)
        )
        above, here = here, below
        if i % LINES == LINES - 1:
            piece = pl.ds(i + 1 - LINES, LINES)
            stores.append(
                pltpu.make_async_copy(out_ref.at[piece], out_hbm.at[piece], sems.at[i // LINES])
            )
            stores[-1].start()
    for store in stores:
        store.wait()


def transport(reacted, up, down, left, right, courant, diffusion):
    shape = reacted.shape
    return pl.pallas_call(
        transport_kernel,
        out_shape=jax.ShapeDtypeStruct(shape, F32),
        in_specs=[pl.BlockSpec(memory_space=pltpu.VMEM)] * 7,
        out_specs=pl.BlockSpec(memory_space=pl.ANY),
        scratch_shapes=[
            pltpu.VMEM(shape, F32),
            pltpu.SemaphoreType.DMA((shape[0] // LINES,)),
        ],
        compiler_params=pltpu.CompilerParams(vmem_limit_bytes=20 << 20),
    )(reacted, up, down, left, right, courant, diffusion)


def shifted(block, axis, ahead):
    count = lax.axis_size(axis)
    forward = [(i, i + 1) for i in range(count - 1)]
    return lax.ppermute(block, axis, forward if ahead else [(j, i) for i, j in forward])


def local(
    state, courant, diffusion, table_value, table_base, table_sens, slot_cell, hit_step, entry_ids
):
    rows_here, cols_here, width = state.shape
    cells = rows_here * cols_here
    nparts = lax.axis_size("blk")
    me = lax.axis_index("blk").astype(jnp.int32).reshape(1)
    flat = state.reshape(cells, width)
    send, code, sens = pack(me, slot_cell[0], hit_step[0], flat, table_sens, nparts)
    recv = lax.all_to_all(send.reshape(nparts, SEG, width), "blk", 0, 0, tiled=True)
    done = react(
        entry_ids, recv.reshape(nparts * SEG, width),
        table_value, table_base, sens, nparts,
    )
    back = lax.all_to_all(done.reshape(nparts, CAP, width), "blk", 0, 0, tiled=True)
    back = back.reshape(nparts * CAP, width)
    last_line, first_line, last_column, first_column = edges(code, back)
    up = shifted(last_line, "grid", True)
    down = shifted(first_line, "grid", False)
    left = shifted(last_column, "blk", True)
    right = shifted(first_column, "blk", False)
    reacted = unpack(code, back).reshape(rows_here, cols_here, width)
    return transport(
        reacted, up, down, left, right, courant.T, diffusion.reshape(1, width)
    )


def solution(mesh):
    return jax.shard_map(
        local,
        mesh=mesh,
        in_specs=(
            P("grid", "blk", None),
            P("grid", "blk"),
            P(),
            P("blk", None),
            P("blk", None),
            P("blk", None, None),
            P("grid", "blk", None),
            P("grid", "blk", None),
            P("blk", "grid", None),
        ),
        out_specs=P("grid", "blk", None),
        check_vma=False,
    )
```

```python
import jax
import jax.numpy as jnp
from jax import lax
from jax.experimental import pallas as pl
from jax.experimental.pallas import tpu as pltpu
from jax.sharding import PartitionSpec as P

F32 = jnp.float32
BF16 = jnp.bfloat16
CAP = 512
META = 16
SEG = CAP + META
WIN = 24
GROUPS = 48
LINES = 4
PARTS = 8
GROUP = 16


def iota(shape, dim):
    return lax.broadcasted_iota(jnp.int32, shape, dim)


def zero_one(mask):
    return jnp.where(mask, 1.0, 0.0).astype(BF16)


def dot(a, b):
    return lax.dot_general(a, b, (((1,), (0,)), ((), ())), preferred_element_type=F32)


def dot_nt(a, b):
    return lax.dot_general(a, b, (((1,), (1,)), ((), ())), preferred_element_type=F32)


def pack_kernel(
    nparts, me_ref, slots_hbm, hits_hbm, state_hbm, sens_hbm, send_ref, back_ref, sens_ref,
    slots_ref, hits_ref, state_ref, field, packed, code_vmem, code_smem, sems,
):
    nblocks, width = slots_ref.shape
    cells = state_ref.shape[0]
    rows_here = cells // width
    loads = [
        pltpu.make_async_copy(slots_hbm, slots_ref, sems.at[0]),
        pltpu.make_async_copy(hits_hbm, hits_ref, sems.at[1]),
        pltpu.make_async_copy(state_hbm, state_ref, sems.at[2]),
    ]
    for load in loads:
        load.start()
    fetch = pltpu.make_async_copy(sens_hbm, sens_ref, sems.at[4])
    fetch.start()
    before = zero_one(iota((width, width), 0) < iota((width, width), 1))
    weights = jnp.concatenate([jnp.ones((width, width), BF16), before], axis=0)
    earlier = zero_one(iota((width, nblocks), 1) < iota((width, nblocks), 0))
    ones = jnp.ones((META, width), BF16)
    top = iota((META, width), 0) == 0
    loads[0].wait()
    loads[1].wait()
    slots = slots_ref[...]
    live = slots >= 0
    owner = jnp.where(live, (hits_ref[...] + me_ref[0]) & (nparts - 1), nparts)
    mine = [owner == part for part in range(nparts)]
    masks = [zero_one(each) for each in mine]
    ahead = [dot(earlier, mask).astype(BF16) for mask in masks]
    ranks = dot(
        jnp.concatenate(
            [jnp.concatenate([a[:nblocks], m], axis=1) for a, m in zip(ahead, masks)], axis=0
        ),
        weights,
    )
    begins = dot_nt(ones, jnp.concatenate(ahead, axis=0))
    place = jnp.zeros((nblocks, width), F32)
    for part in range(nparts):
        place = place + jnp.where(mine[part], ranks[part * nblocks : (part + 1) * nblocks], 0.0)
        begin = begins[:, part * width : (part + 1) * width]
        high = jnp.floor(begin * (1.0 / 16.0))
        send_ref[pl.ds(part * SEG + CAP, META), :] = jnp.where(
            top, high, begin - 16.0 * high
        ).astype(BF16)
    spot = owner * CAP + place.astype(jnp.int32)
    spot_high = (spot >> 7).astype(F32)
    spot_low = (spot & 127).astype(F32)
    cell_row = slots >> 7
    cell_col = slots & 127
    total = jnp.zeros((2 * rows_here, width), F32)
    row_ids = iota((rows_here, width), 0)
    col_ids = iota((width, width), 0)
    for pair in range(0, nblocks, 2):
        lhs, rhs = [], []
        for k in (pair, pair + 1):
            at_row = row_ids == cell_row[k : k + 1, :]
            lhs.append(
                jnp.concatenate(
                    [
                        jnp.where(at_row, spot_high[k : k + 1, :], 0.0),
                        jnp.where(at_row, spot_low[k : k + 1, :], 0.0),
                    ],
                    axis=0,
                ).astype(BF16)
            )
            rhs.append(zero_one(col_ids == cell_col[k : k + 1, :]))
        total = total + dot_nt(jnp.concatenate(lhs, axis=1), jnp.concatenate(rhs, axis=1))
    back = (total[:rows_here] * 128.0 + total[rows_here:]).astype(jnp.int32)
    back_ref[...] = back
    code_vmem[...] = back + (back >> 9) * META
    copy = pltpu.make_async_copy(code_vmem, code_smem, sems.at[3])
    copy.start()
    loads[2].wait()
    field[...] = state_ref[...].astype(F32)
    copy.wait()

    def line(i, _):
        for q in range(0, width, GROUP):
            values = [field[pl.ds(i * width + q + j, 1), :] for j in range(GROUP)]
            spots = [code_smem[i, q + j] for j in range(GROUP)]
            for value, at in zip(values, spots):
                packed[pl.ds(at, 1), :] = value
        return 0

    lax.fori_loop(0, rows_here, line, 0)
    for part in range(nparts):
        send_ref[pl.ds(part * SEG, CAP), :] = packed[pl.ds(part * SEG, CAP), :].astype(BF16)
    fetch.wait()


def pack(me, slots, hits, flat, sens, nparts):
    nblocks, width = slots.shape
    cells = flat.shape[0]
    return pl.pallas_call(
        lambda *refs: pack_kernel(nparts, *refs),
        out_shape=(
            jax.ShapeDtypeStruct((nparts * SEG, width), BF16),
            jax.ShapeDtypeStruct((cells // width, width), jnp.int32),
            pltpu.VMEM(sens.shape, BF16),
        ),
        in_specs=[pl.BlockSpec(memory_space=pltpu.SMEM)]
        + [pl.BlockSpec(memory_space=pltpu.HBM)] * 4,
        out_specs=[pl.BlockSpec(memory_space=pltpu.VMEM)] * 3,
        scratch_shapes=[
            pltpu.VMEM((nblocks, width), jnp.int32),
            pltpu.VMEM((nblocks, width), jnp.int32),
            pltpu.VMEM((cells, width), BF16),
            pltpu.VMEM((cells, width), F32),
            pltpu.VMEM((nparts * SEG, width), F32),
            pltpu.VMEM((cells // width, width), jnp.int32),
            pltpu.SMEM((cells // width, width), jnp.int32),
            pltpu.SemaphoreType.DMA((5,)),
        ],
        compiler_params=pltpu.CompilerParams(vmem_limit_bytes=36 << 20),
    )(me, *[pltpu.with_memory_space_constraint(each, pltpu.HBM) for each in (slots, hits, flat, sens)])


def react_kernel(
    nparts, nblocks, entries_ref, recv_ref, value_ref, base_ref, sens_ref, out_ref,
    rows, mapped, table, begin_vmem, begin_smem, sem,
):
    width = recv_ref.shape[1]
    depth = base_ref.shape[0]
    for part in range(nparts):
        meta = recv_ref[pl.ds(part * SEG + CAP, META), :].astype(F32)
        begin_vmem[pl.ds(part, 1), :] = (meta[0:1] * 16.0 + meta[1:2]).astype(jnp.int32)
    begin = begin_vmem[pl.ds(0, nparts), :]
    lane = iota((nparts, width), 1)
    counts = pltpu.roll(begin, width - 1, 1) - begin
    end = width - 1
    following = jnp.where((lane < nblocks) & (counts > WIN), lane, end)
    ahead = 1
    while ahead < width:
        moved = pltpu.roll(following, width - ahead, 1)
        following = jnp.minimum(following, jnp.where(lane + ahead < width, moved, end))
        ahead *= 2
    begin_vmem[pl.ds(0, nparts), :] = begin + SEG * iota((nparts, width), 0)
    begin_vmem[pl.ds(nparts, nparts), :] = pltpu.roll(following, end, 1)
    copy = pltpu.make_async_copy(begin_vmem, begin_smem, sem)
    copy.start()
    table[pl.ds(0, depth), :] = base_ref[...].astype(F32)
    table[pl.ds(depth, depth), :] = value_ref[...].astype(F32)

    def widen(part, _):
        at = pl.multiple_of(part * SEG, 16)
        rows[pl.ds(at, SEG), :] = recv_ref[pl.ds(at, SEG), :].astype(F32)
        return 0

    lax.fori_loop(0, nparts, widen, 0)
    copy.wait()

    def delta(at, entry):
        base = table[pl.ds(entry, 1), :]
        return rows[pl.ds(at, WIN), :] - base

    def batch(part, first):
        at = [begin_smem[part, first + i] for i in range(GROUPS + 1)]
        entry = [entries_ref[0, 0, part * nblocks + first + i] for i in range(GROUPS)]
        dx = [delta(at[i], entry[i]) for i in range(GROUPS)]
        results = []
        for i in range(0, GROUPS, 2):
            product = dot(
                jnp.concatenate([dx[i], dx[i + 1]], axis=0).astype(BF16),
                jnp.concatenate([sens_ref[entry[i]], sens_ref[entry[i + 1]]], axis=1),
            )
            results.append(product[:WIN, :width] + table[pl.ds(entry[i] + depth, 1), :])
            results.append(product[WIN:, width:] + table[pl.ds(entry[i + 1] + depth, 1), :])
        for i in range(GROUPS):
            mapped[pl.ds(at[i], WIN), :] = results[i]

    def sources(step, _):
        for i in range(PARTS):
            batch(step * PARTS + i, 0)
        return 0

    lax.fori_loop(0, nparts // PARTS, sources, 0)

    def rest(part, _):
        def group(k):
            entry = entries_ref[0, 0, part * nblocks + k]
            at, stop = begin_smem[part, k], begin_smem[part, k + 1]

            def more(here):
                result = dot(delta(here, entry).astype(BF16), sens_ref[entry])
                result = result + table[pl.ds(entry + depth, 1), :]
                mapped[pl.ds(here, WIN), :] = jnp.where(
                    iota((WIN, width), 0) < stop - here, result, mapped[pl.ds(here, WIN), :]
                )
                return here + WIN

            lax.while_loop(lambda here: here < stop, more, at + WIN)
            return begin_smem[nparts + part, k]

        lax.while_loop(lambda k: k < end, group, begin_smem[nparts + part, end])
        return 0

    lax.fori_loop(0, nparts, rest, 0)

    def narrow(part, _):
        out_ref[pl.ds(pl.multiple_of(part * CAP, 16), CAP), :] = mapped[
            pl.ds(pl.multiple_of(part * SEG, 16), CAP), :
        ].astype(BF16)
        return 0

    lax.fori_loop(0, nparts, narrow, 0)


def react(entries, recv, value, base, sens, nparts):
    width = recv.shape[1]
    nblocks = entries.shape[-1] // nparts
    return pl.pallas_call(
        lambda *refs: react_kernel(nparts, nblocks, *refs),
        out_shape=jax.ShapeDtypeStruct((nparts * CAP, width), BF16),
        in_specs=[pl.BlockSpec(memory_space=pltpu.SMEM)]
        + [pl.BlockSpec(memory_space=pltpu.VMEM)] * 4,
        out_specs=pl.BlockSpec(memory_space=pltpu.VMEM),
        scratch_shapes=[
            pltpu.VMEM((nparts * SEG + WIN, width), F32),
            pltpu.VMEM((nparts * SEG + WIN, width), F32),
            pltpu.VMEM((2 * base.shape[0], width), F32),
            pltpu.VMEM((2 * nparts, width), jnp.int32),
            pltpu.SMEM((2 * nparts, width), jnp.int32),
            pltpu.SemaphoreType.DMA,
        ],
        compiler_params=pltpu.CompilerParams(vmem_limit_bytes=24 << 20),
    )(entries, recv, value, base, sens)


def edges_kernel(code_ref, ret_ref, up_ref, down_ref, left_ref, right_ref, rows):
    rows_here, width = code_ref.shape
    cols_here = width
    rows[...] = ret_ref[...].astype(F32)

    def gather(out, spots):
        for first in range(0, len(spots), GROUP):
            out[pl.ds(first, GROUP), :] = jnp.concatenate(
                [rows[pl.ds(at, 1), :] for at in spots[first : first + GROUP]], axis=0
            ).astype(BF16)

    gather(up_ref, [code_ref[rows_here - 1, j] for j in range(cols_here)])
    gather(down_ref, [code_ref[0, j] for j in range(cols_here)])
    gather(left_ref, [code_ref[i, cols_here - 1] for i in range(rows_here)])
    gather(right_ref, [code_ref[i, 0] for i in range(rows_here)])


def edges(code, ret):
    rows_here, width = code.shape
    ends = [rows_here if side else width for side in (0, 0, 1, 1)]
    return pl.pallas_call(
        edges_kernel,
        out_shape=[jax.ShapeDtypeStruct((end, width), BF16) for end in ends],
        in_specs=[
            pl.BlockSpec(memory_space=pltpu.SMEM),
            pl.BlockSpec(memory_space=pltpu.VMEM),
        ],
        out_specs=[pl.BlockSpec(memory_space=pltpu.VMEM)] * 4,
        scratch_shapes=[pltpu.VMEM(ret.shape, F32)],
        compiler_params=pltpu.CompilerParams(vmem_limit_bytes=20 << 20),
    )(code, ret)


def unpack_kernel(code_ref, ret_ref, out_ref, rows):
    rows_here, width = code_ref.shape
    rows[...] = ret_ref[...].astype(F32)

    def line(i, _):
        for q in range(0, width, GROUP):
            spots = [code_ref[i, q + j] for j in range(GROUP)]
            values = [rows[pl.ds(at, 1), :] for at in spots]
            for j, value in enumerate(values):
                out_ref[pl.ds(i * width + q + j, 1), :] = value
        return 0

    lax.fori_loop(0, rows_here, line, 0)


def unpack(code, ret):
    cells, width = code.size, ret.shape[1]
    return pl.pallas_call(
        unpack_kernel,
        out_shape=jax.ShapeDtypeStruct((cells, width), F32),
        in_specs=[
            pl.BlockSpec(memory_space=pltpu.SMEM),
            pl.BlockSpec(memory_space=pltpu.VMEM),
        ],
        out_specs=pl.BlockSpec(memory_space=pltpu.VMEM),
        scratch_shapes=[pltpu.VMEM(ret.shape, F32)],
        compiler_params=pltpu.CompilerParams(vmem_limit_bytes=20 << 20),
        cost_estimate=pl.CostEstimate(flops=0, bytes_accessed=16 << 20, transcendentals=0),
    )(code, ret)


def transport_kernel(
    mid_ref, up_ref, down_ref, left_ref, right_ref, courant_ref, diffusion_ref, out_hbm,
    out_ref, sems,
):
    rows_here, cols, width = mid_ref.shape
    diffusion = diffusion_ref[...]
    first = iota((cols, width), 0) == 0
    last = iota((cols, width), 0) == cols - 1

    def row(i):
        if i < 0:
            return up_ref[...].astype(F32)
        if i >= rows_here:
            return down_ref[...].astype(F32)
        return mid_ref[i]

    stores = []
    above, here = row(-1), row(0)
    for i in range(rows_here):
        below = row(i + 1)
        left = jnp.where(first, left_ref[i : i + 1, :].astype(F32), pltpu.roll(here, 1, 0))
        right = jnp.where(
            last, right_ref[i : i + 1, :].astype(F32), pltpu.roll(here, cols - 1, 0)
        )
        courant = courant_ref[:, i : i + 1]
        out_ref[i] = (
            here
            - courant * (here - above)
            + diffusion * (above + below + left + right - 4.0 * here)
        )
        above, here = here, below
        if i % LINES == LINES - 1:
            piece = pl.ds(i + 1 - LINES, LINES)
            stores.append(
                pltpu.make_async_copy(out_ref.at[piece], out_hbm.at[piece], sems.at[i // LINES])
            )
            stores[-1].start()
    for store in stores:
        store.wait()


def transport(reacted, up, down, left, right, courant, diffusion):
    shape = reacted.shape
    return pl.pallas_call(
        transport_kernel,
        out_shape=jax.ShapeDtypeStruct(shape, F32),
        in_specs=[pl.BlockSpec(memory_space=pltpu.VMEM)] * 7,
        out_specs=pl.BlockSpec(memory_space=pl.ANY),
        scratch_shapes=[
            pltpu.VMEM(shape, F32),
            pltpu.SemaphoreType.DMA((shape[0] // LINES,)),
        ],
        compiler_params=pltpu.CompilerParams(vmem_limit_bytes=20 << 20),
    )(reacted, up, down, left, right, courant, diffusion)


def shifted(block, axis, ahead):
    count = lax.axis_size(axis)
    forward = [(i, i + 1) for i in range(count - 1)]
    return lax.ppermute(block, axis, forward if ahead else [(j, i) for i, j in forward])


def local(
    state, courant, diffusion, table_value, table_base, table_sens, slot_cell, hit_step, entry_ids
):
    rows_here, cols_here, width = state.shape
    cells = rows_here * cols_here
    nparts = lax.axis_size("blk")
    me = lax.axis_index("blk").astype(jnp.int32).reshape(1)
    flat = state.reshape(cells, width)
    send, code, sens = pack(me, slot_cell[0], hit_step[0], flat, table_sens, nparts)
    recv = lax.all_to_all(send.reshape(nparts, SEG, width), "blk", 0, 0, tiled=True)
    done = react(
        entry_ids, recv.reshape(nparts * SEG, width),
        table_value, table_base, sens, nparts,
    )
    back = lax.all_to_all(done.reshape(nparts, CAP, width), "blk", 0, 0, tiled=True)
    back = back.reshape(nparts * CAP, width)
    last_line, first_line, last_column, first_column = edges(code, back)
    up = shifted(last_line, "grid", True)
    down = shifted(first_line, "grid", False)
    left = shifted(last_column, "blk", True)
    right = shifted(first_column, "blk", False)
    reacted = unpack(code, back).reshape(rows_here, cols_here, width)
    return transport(
        reacted, up, down, left, right, courant.T, diffusion.reshape(1, width)
    )


def solution(mesh):
    return jax.shard_map(
        local,
        mesh=mesh,
        in_specs=(
            P("grid", "blk", None),
            P("grid", "blk"),
            P(),
            P("blk", None),
            P("blk", None),
            P("blk", None, None),
            P("grid", "blk", None),
            P("grid", "blk", None),
            P("blk", "grid", None),
        ),
        out_specs=P("grid", "blk", None),
        check_vma=False,
    )
```

```python
import jax
import jax.numpy as jnp
from jax import lax
from jax.experimental import pallas as pl
from jax.experimental.pallas import tpu as pltpu
from jax.sharding import PartitionSpec as P

F32 = jnp.float32
BF16 = jnp.bfloat16
CAP = 512
META = 16
SEG = CAP + META
WIN = 24
GROUPS = 48
STEP = 4
PARTS = 8
GROUP = 16


def iota(shape, dim):
    return lax.broadcasted_iota(jnp.int32, shape, dim)


def zero_one(mask):
    return jnp.where(mask, 1.0, 0.0).astype(BF16)


def dot(a, b):
    return lax.dot_general(a, b, (((1,), (0,)), ((), ())), preferred_element_type=F32)


def dot_nt(a, b):
    return lax.dot_general(a, b, (((1,), (1,)), ((), ())), preferred_element_type=F32)


def pack_kernel(
    nparts, lines, me_ref, slots_hbm, hits_hbm, state_hbm, sens_hbm, send_ref, back_ref, sens_ref,
    slots_ref, hits_ref, state_ref, field, packed, code_vmem, code_smem, sems,
):
    nblocks, width = slots_ref.shape
    cells = state_ref.shape[0]
    rows_here = cells // width
    loads = [
        pltpu.make_async_copy(slots_hbm, slots_ref, sems.at[0]),
        pltpu.make_async_copy(hits_hbm, hits_ref, sems.at[1]),
        pltpu.make_async_copy(state_hbm, state_ref, sems.at[2]),
    ]
    for load in loads:
        load.start()
    fetch = pltpu.make_async_copy(sens_hbm, sens_ref, sems.at[4])
    fetch.start()
    before = zero_one(iota((width, width), 0) < iota((width, width), 1))
    weights = jnp.concatenate([jnp.ones((width, width), BF16), before], axis=0)
    earlier = zero_one(iota((width, nblocks), 1) < iota((width, nblocks), 0))
    ones = jnp.ones((META, width), BF16)
    top = iota((META, width), 0) == 0
    loads[0].wait()
    loads[1].wait()
    slots = slots_ref[...]
    live = slots >= 0
    owner = jnp.where(live, (hits_ref[...] + (me_ref[0] // lines)) & (nparts - 1), nparts)
    mine = [owner == part for part in range(nparts)]
    masks = [zero_one(each) for each in mine]
    ahead = [dot(earlier, mask).astype(BF16) for mask in masks]
    ranks = dot(
        jnp.concatenate(
            [jnp.concatenate([a[:nblocks], m], axis=1) for a, m in zip(ahead, masks)], axis=0
        ),
        weights,
    )
    begins = dot_nt(ones, jnp.concatenate(ahead, axis=0))
    place = jnp.zeros((nblocks, width), F32)
    for part in range(nparts):
        place = place + jnp.where(mine[part], ranks[part * nblocks : (part + 1) * nblocks], 0.0)
        begin = begins[:, part * width : (part + 1) * width]
        high = jnp.floor(begin * (1.0 / 16.0))
        send_ref[pl.ds(part * SEG + CAP, META), :] = jnp.where(
            top, high, begin - 16.0 * high
        ).astype(BF16)
    spot = owner * CAP + place.astype(jnp.int32)
    spot_high = (spot >> 7).astype(F32)
    spot_low = (spot & 127).astype(F32)
    cell_row = slots >> 7
    cell_col = slots & 127
    total = jnp.zeros((2 * rows_here, width), F32)
    row_ids = iota((rows_here, width), 0)
    col_ids = iota((width, width), 0)
    for pair in range(0, nblocks, 2):
        lhs, rhs = [], []
        for k in (pair, pair + 1):
            at_row = row_ids == cell_row[k : k + 1, :]
            lhs.append(
                jnp.concatenate(
                    [
                        jnp.where(at_row, spot_high[k : k + 1, :], 0.0),
                        jnp.where(at_row, spot_low[k : k + 1, :], 0.0),
                    ],
                    axis=0,
                ).astype(BF16)
            )
            rhs.append(zero_one(col_ids == cell_col[k : k + 1, :]))
        total = total + dot_nt(jnp.concatenate(lhs, axis=1), jnp.concatenate(rhs, axis=1))
    back = (total[:rows_here] * 128.0 + total[rows_here:]).astype(jnp.int32)
    back_ref[...] = back
    code_vmem[...] = back + (back >> 9) * META
    copy = pltpu.make_async_copy(code_vmem, code_smem, sems.at[3])
    copy.start()
    loads[2].wait()
    field[...] = state_ref[...].astype(F32)
    copy.wait()

    def line(i, _):
        for q in range(0, width, GROUP):
            values = [field[pl.ds(i * width + q + j, 1), :] for j in range(GROUP)]
            spots = [code_smem[i, q + j] for j in range(GROUP)]
            for value, at in zip(values, spots):
                packed[pl.ds(at, 1), :] = value
        return 0

    lax.fori_loop(0, rows_here, line, 0)
    for part in range(nparts):
        send_ref[pl.ds(part * SEG, CAP), :] = packed[pl.ds(part * SEG, CAP), :].astype(BF16)
    fetch.wait()


def pack(me, slots, hits, flat, sens, nparts, lines):
    nblocks, width = slots.shape
    cells = flat.shape[0]
    return pl.pallas_call(
        lambda *refs: pack_kernel(nparts, lines, *refs),
        out_shape=(
            jax.ShapeDtypeStruct((nparts * SEG, width), BF16),
            jax.ShapeDtypeStruct((cells // width, width), jnp.int32),
            pltpu.VMEM(sens.shape, BF16),
        ),
        in_specs=[pl.BlockSpec(memory_space=pltpu.SMEM)]
        + [pl.BlockSpec(memory_space=pltpu.HBM)] * 4,
        out_specs=[pl.BlockSpec(memory_space=pltpu.VMEM)] * 3,
        scratch_shapes=[
            pltpu.VMEM((nblocks, width), jnp.int32),
            pltpu.VMEM((nblocks, width), jnp.int32),
            pltpu.VMEM((cells, width), BF16),
            pltpu.VMEM((cells, width), F32),
            pltpu.VMEM((nparts * SEG, width), F32),
            pltpu.VMEM((cells // width, width), jnp.int32),
            pltpu.SMEM((cells // width, width), jnp.int32),
            pltpu.SemaphoreType.DMA((5,)),
        ],
        compiler_params=pltpu.CompilerParams(vmem_limit_bytes=36 << 20),
    )(me, *[pltpu.with_memory_space_constraint(each, pltpu.HBM) for each in (slots, hits, flat, sens)])


def react_kernel(
    nparts, nblocks, entries_ref, recv_ref, value_ref, base_ref, sens_ref, out_ref,
    rows, mapped, table, begin_vmem, begin_smem, sem,
):
    width = recv_ref.shape[1]
    depth = base_ref.shape[0]
    for part in range(nparts):
        meta = recv_ref[pl.ds(part * SEG + CAP, META), :].astype(F32)
        begin_vmem[pl.ds(part, 1), :] = (meta[0:1] * 16.0 + meta[1:2]).astype(jnp.int32)
    begin = begin_vmem[pl.ds(0, nparts), :]
    lane = iota((nparts, width), 1)
    counts = pltpu.roll(begin, width - 1, 1) - begin
    end = width - 1
    following = jnp.where((lane < nblocks) & (counts > WIN), lane, end)
    ahead = 1
    while ahead < width:
        moved = pltpu.roll(following, width - ahead, 1)
        following = jnp.minimum(following, jnp.where(lane + ahead < width, moved, end))
        ahead *= 2
    begin_vmem[pl.ds(0, nparts), :] = begin + SEG * iota((nparts, width), 0)
    begin_vmem[pl.ds(nparts, nparts), :] = pltpu.roll(following, end, 1)
    copy = pltpu.make_async_copy(begin_vmem, begin_smem, sem)
    copy.start()
    table[pl.ds(0, depth), :] = base_ref[...].astype(F32)
    table[pl.ds(depth, depth), :] = value_ref[...].astype(F32)

    def widen(part, _):
        at = pl.multiple_of(part * SEG, 16)
        rows[pl.ds(at, SEG), :] = recv_ref[pl.ds(at, SEG), :].astype(F32)
        return 0

    lax.fori_loop(0, nparts, widen, 0)
    copy.wait()

    def delta(at, entry):
        base = table[pl.ds(entry, 1), :]
        return rows[pl.ds(at, WIN), :] - base

    def batch(part, first):
        at = [begin_smem[part, first + i] for i in range(GROUPS + 1)]
        entry = [entries_ref[0, 0, part * nblocks + first + i] for i in range(GROUPS)]
        dx = [delta(at[i], entry[i]) for i in range(GROUPS)]
        results = []
        for i in range(0, GROUPS, 2):
            product = dot(
                jnp.concatenate([dx[i], dx[i + 1]], axis=0).astype(BF16),
                jnp.concatenate([sens_ref[entry[i]], sens_ref[entry[i + 1]]], axis=1),
            )
            results.append(product[:WIN, :width] + table[pl.ds(entry[i] + depth, 1), :])
            results.append(product[WIN:, width:] + table[pl.ds(entry[i + 1] + depth, 1), :])
        for i in range(GROUPS):
            mapped[pl.ds(at[i], WIN), :] = results[i]

    def sources(step, _):
        for i in range(PARTS):
            batch(step * PARTS + i, 0)
        return 0

    lax.fori_loop(0, nparts // PARTS, sources, 0)

    def rest(part, _):
        def group(k):
            entry = entries_ref[0, 0, part * nblocks + k]
            at, stop = begin_smem[part, k], begin_smem[part, k + 1]

            def more(here):
                result = dot(delta(here, entry).astype(BF16), sens_ref[entry])
                result = result + table[pl.ds(entry + depth, 1), :]
                mapped[pl.ds(here, WIN), :] = jnp.where(
                    iota((WIN, width), 0) < stop - here, result, mapped[pl.ds(here, WIN), :]
                )
                return here + WIN

            lax.while_loop(lambda here: here < stop, more, at + WIN)
            return begin_smem[nparts + part, k]

        lax.while_loop(lambda k: k < end, group, begin_smem[nparts + part, end])
        return 0

    lax.fori_loop(0, nparts, rest, 0)

    def narrow(part, _):
        out_ref[pl.ds(pl.multiple_of(part * CAP, 16), CAP), :] = mapped[
            pl.ds(pl.multiple_of(part * SEG, 16), CAP), :
        ].astype(BF16)
        return 0

    lax.fori_loop(0, nparts, narrow, 0)


def react(entries, recv, value, base, sens, nparts):
    width = recv.shape[1]
    nblocks = entries.shape[-1] // nparts
    return pl.pallas_call(
        lambda *refs: react_kernel(nparts, nblocks, *refs),
        out_shape=jax.ShapeDtypeStruct((nparts * CAP, width), BF16),
        in_specs=[pl.BlockSpec(memory_space=pltpu.SMEM)]
        + [pl.BlockSpec(memory_space=pltpu.VMEM)] * 4,
        out_specs=pl.BlockSpec(memory_space=pltpu.VMEM),
        scratch_shapes=[
            pltpu.VMEM((nparts * SEG + WIN, width), F32),
            pltpu.VMEM((nparts * SEG + WIN, width), F32),
            pltpu.VMEM((2 * base.shape[0], width), F32),
            pltpu.VMEM((2 * nparts, width), jnp.int32),
            pltpu.SMEM((2 * nparts, width), jnp.int32),
            pltpu.SemaphoreType.DMA,
        ],
        compiler_params=pltpu.CompilerParams(vmem_limit_bytes=24 << 20),
    )(entries, recv, value, base, sens)


def edges_kernel(
    lines, me_ref, code_ref, ret_ref, along1_ref, along2_ref, across1_ref, across2_ref, rows
):
    rows_here, width = code_ref.shape
    cols_here = width
    rows[...] = ret_ref[...].astype(F32)
    along, across = me_ref[0] & 1, (me_ref[0] // lines) & 1

    def gather(out, spots):
        for first in range(0, len(spots), GROUP):
            out[pl.ds(first, GROUP), :] = jnp.concatenate(
                [rows[pl.ds(at, 1), :] for at in spots[first : first + GROUP]], axis=0
            ).astype(BF16)

    for out, line in (
        (along1_ref, (1 - along) * (rows_here - 1)),
        (along2_ref, along * (rows_here - 1)),
    ):
        gather(out, [code_ref[line, j] for j in range(cols_here)])
    for out, column in (
        (across1_ref, (1 - across) * (cols_here - 1)),
        (across2_ref, across * (cols_here - 1)),
    ):
        gather(out, [code_ref[i, column] for i in range(rows_here)])


def edges(me, code, ret, lines):
    rows_here, width = code.shape
    ends = [rows_here if side else width for side in (0, 0, 1, 1)]
    return pl.pallas_call(
        lambda *refs: edges_kernel(lines, *refs),
        out_shape=[jax.ShapeDtypeStruct((end, width), BF16) for end in ends],
        in_specs=[pl.BlockSpec(memory_space=pltpu.SMEM)] * 2
        + [pl.BlockSpec(memory_space=pltpu.VMEM)],
        out_specs=[pl.BlockSpec(memory_space=pltpu.VMEM)] * 4,
        scratch_shapes=[pltpu.VMEM(ret.shape, F32)],
        compiler_params=pltpu.CompilerParams(vmem_limit_bytes=20 << 20),
    )(me, code, ret)


def unpack_kernel(code_ref, ret_ref, out_ref, rows):
    rows_here, width = code_ref.shape
    rows[...] = ret_ref[...].astype(F32)

    def line(i, _):
        for q in range(0, width, GROUP):
            spots = [code_ref[i, q + j] for j in range(GROUP)]
            values = [rows[pl.ds(at, 1), :] for at in spots]
            for j, value in enumerate(values):
                out_ref[pl.ds(i * width + q + j, 1), :] = value
        return 0

    lax.fori_loop(0, rows_here, line, 0)


def unpack(code, ret):
    cells, width = code.size, ret.shape[1]
    return pl.pallas_call(
        unpack_kernel,
        out_shape=jax.ShapeDtypeStruct((cells, width), F32),
        in_specs=[
            pl.BlockSpec(memory_space=pltpu.SMEM),
            pl.BlockSpec(memory_space=pltpu.VMEM),
        ],
        out_specs=pl.BlockSpec(memory_space=pltpu.VMEM),
        scratch_shapes=[pltpu.VMEM(ret.shape, F32)],
        compiler_params=pltpu.CompilerParams(vmem_limit_bytes=20 << 20),
        cost_estimate=pl.CostEstimate(flops=0, bytes_accessed=16 << 20, transcendentals=0),
    )(code, ret)


def transport_kernel(
    lines, me_ref, mid_ref, along1_ref, along2_ref, across1_ref, across2_ref,
    courant_ref, diffusion_ref, out_hbm, out_ref, sems,
):
    rows_here, cols, width = mid_ref.shape

    def sides(odd, one, two):
        one, two = one[...].astype(F32), two[...].astype(F32)
        return jnp.where(odd == 1, one, two), jnp.where(odd == 1, two, one)

    up, down = sides(me_ref[0] & 1, along1_ref, along2_ref)
    left_side, right_side = sides((me_ref[0] // lines) & 1, across1_ref, across2_ref)
    diffusion = diffusion_ref[...]
    first = iota((cols, width), 0) == 0
    last = iota((cols, width), 0) == cols - 1

    def row(i):
        if i < 0:
            return up
        if i >= rows_here:
            return down
        return mid_ref[i]

    stores = []
    above, here = row(-1), row(0)
    for i in range(rows_here):
        below = row(i + 1)
        left = jnp.where(first, left_side[i : i + 1, :], pltpu.roll(here, 1, 0))
        right = jnp.where(
            last, right_side[i : i + 1, :], pltpu.roll(here, cols - 1, 0)
        )
        courant = courant_ref[:, i : i + 1]
        out_ref[i] = (
            here
            - courant * (here - above)
            + diffusion * (above + below + left + right - 4.0 * here)
        )
        above, here = here, below
        if i % STEP == STEP - 1:
            piece = pl.ds(i + 1 - STEP, STEP)
            stores.append(
                pltpu.make_async_copy(out_ref.at[piece], out_hbm.at[piece], sems.at[i // STEP])
            )
            stores[-1].start()
    for store in stores:
        store.wait()


def transport(me, lines, reacted, halo, courant, diffusion):
    shape = reacted.shape
    return pl.pallas_call(
        lambda *refs: transport_kernel(lines, *refs),
        out_shape=jax.ShapeDtypeStruct(shape, F32),
        in_specs=[pl.BlockSpec(memory_space=pltpu.SMEM)]
        + [pl.BlockSpec(memory_space=pltpu.VMEM)] * 7,
        out_specs=pl.BlockSpec(memory_space=pl.ANY),
        scratch_shapes=[
            pltpu.VMEM(shape, F32),
            pltpu.SemaphoreType.DMA((shape[0] // STEP,)),
        ],
        compiler_params=pltpu.CompilerParams(vmem_limit_bytes=20 << 20),
    )(me, reacted, *halo, courant, diffusion)


def swapped(block, axis, first):
    pairs = [(i, i + 1) for i in range(first, lax.axis_size(axis) - 1, 2)]
    return lax.ppermute(block, axis, pairs + [(j, i) for i, j in pairs])


def local(
    state, courant, diffusion, table_value, table_base, table_sens, slot_cell, hit_step, entry_ids
):
    rows_here, cols_here, width = state.shape
    cells = rows_here * cols_here
    nparts, lines = lax.axis_size("blk"), lax.axis_size("grid")
    me = lax.axis_index(("blk", "grid")).astype(jnp.int32).reshape(1)
    flat = state.reshape(cells, width)
    send, code, sens = pack(me, slot_cell[0], hit_step[0], flat, table_sens, nparts, lines)
    recv = lax.all_to_all(send.reshape(nparts, SEG, width), "blk", 0, 0, tiled=True)
    done = react(
        entry_ids, recv.reshape(nparts * SEG, width),
        table_value, table_base, sens, nparts,
    )
    back = lax.all_to_all(done.reshape(nparts, CAP, width), "blk", 0, 0, tiled=True)
    back = back.reshape(nparts * CAP, width)
    along1, along2, across1, across2 = edges(me, code, back, lines)
    halo = (
        swapped(along1, "grid", 0), swapped(along2, "grid", 1),
        swapped(across1, "blk", 0), swapped(across2, "blk", 1),
    )
    reacted = unpack(code, back).reshape(rows_here, cols_here, width)
    return transport(me, lines, reacted, halo, courant.T, diffusion.reshape(1, width))


def solution(mesh):
    return jax.shard_map(
        local,
        mesh=mesh,
        in_specs=(
            P("grid", "blk", None),
            P("grid", "blk"),
            P(),
            P("blk", None),
            P("blk", None),
            P("blk", None, None),
            P("grid", "blk", None),
            P("grid", "blk", None),
            P("blk", "grid", None),
        ),
        out_specs=P("grid", "blk", None),
        check_vma=False,
    )
```

```python
import jax
import jax.numpy as jnp
from jax import lax
from jax.experimental import pallas as pl
from jax.experimental.pallas import tpu as pltpu
from jax.sharding import PartitionSpec as P

F32 = jnp.float32
BF16 = jnp.bfloat16
CAP = 512
META = 16
SEG = CAP + META
WIN = 24
GROUPS = 48
STEP = 4
PARTS = 8
GROUP = 16


def iota(shape, dim):
    return lax.broadcasted_iota(jnp.int32, shape, dim)


def zero_one(mask):
    return jnp.where(mask, 1.0, 0.0).astype(BF16)


def dot(a, b):
    return lax.dot_general(a, b, (((1,), (0,)), ((), ())), preferred_element_type=F32)


def dot_nt(a, b):
    return lax.dot_general(a, b, (((1,), (1,)), ((), ())), preferred_element_type=F32)


def pack_kernel(
    nparts, lines, me_ref, slots_hbm, hits_hbm, state_hbm, sens_hbm, send_ref, back_ref, sens_ref,
    slots_ref, hits_ref, state_ref, field, packed, code_vmem, code_smem, sems,
):
    nblocks, width = slots_ref.shape
    cells = state_ref.shape[0]
    rows_here = cells // width
    loads = [
        pltpu.make_async_copy(slots_hbm, slots_ref, sems.at[0]),
        pltpu.make_async_copy(hits_hbm, hits_ref, sems.at[1]),
        pltpu.make_async_copy(state_hbm, state_ref, sems.at[2]),
    ]
    for load in loads:
        load.start()
    fetch = pltpu.make_async_copy(sens_hbm, sens_ref, sems.at[4])
    fetch.start()
    before = zero_one(iota((width, width), 0) < iota((width, width), 1))
    weights = jnp.concatenate([jnp.ones((width, width), BF16), before], axis=0)
    earlier = zero_one(iota((nblocks, nblocks), 1) < iota((nblocks, nblocks), 0))
    starts = zero_one(iota((nblocks, width), 0) < iota((nblocks, width), 1))
    ones = jnp.ones((META, width), BF16)
    top = iota((META, width), 0) == 0
    loads[0].wait()
    loads[1].wait()
    slots = slots_ref[...]
    live = slots >= 0
    owner = jnp.where(live, (hits_ref[...] + (me_ref[0] // lines)) & (nparts - 1), nparts)
    mine = [owner == part for part in range(nparts)]
    masks = [zero_one(each) for each in mine]
    ahead = [dot(earlier, mask).astype(BF16) for mask in masks]
    ranks = dot(
        jnp.concatenate(
            [jnp.concatenate([a, m], axis=1) for a, m in zip(ahead, masks)], axis=0
        ),
        weights,
    )
    place = jnp.zeros((nblocks, width), F32)
    for part in range(nparts):
        place = place + jnp.where(mine[part], ranks[part * nblocks : (part + 1) * nblocks], 0.0)
    spot = owner * CAP + place.astype(jnp.int32)
    spot_high = (spot >> 7).astype(F32)
    spot_low = (spot & 127).astype(F32)
    cell_row = slots >> 7
    cell_col = slots & 127
    total = jnp.zeros((2 * rows_here, width), F32)
    row_ids = iota((rows_here, width), 0)
    col_ids = iota((width, width), 0)
    for pair in range(0, nblocks, 2):
        lhs, rhs = [], []
        for k in (pair, pair + 1):
            at_row = row_ids == cell_row[k : k + 1, :]
            lhs.append(
                jnp.concatenate(
                    [
                        jnp.where(at_row, spot_high[k : k + 1, :], 0.0),
                        jnp.where(at_row, spot_low[k : k + 1, :], 0.0),
                    ],
                    axis=0,
                ).astype(BF16)
            )
            rhs.append(zero_one(col_ids == cell_col[k : k + 1, :]))
        total = total + dot_nt(jnp.concatenate(lhs, axis=1), jnp.concatenate(rhs, axis=1))
    back = (total[:rows_here] * 128.0 + total[rows_here:]).astype(jnp.int32)
    back_ref[...] = back
    code_vmem[...] = back + (back >> 9) * META
    copy = pltpu.make_async_copy(code_vmem, code_smem, sems.at[3])
    copy.start()
    counts = jnp.concatenate([dot_nt(ones, mask) for mask in masks], axis=0).astype(BF16)
    begins = dot(counts, starts)
    for part in range(nparts):
        begin = begins[part * META : (part + 1) * META]
        high = jnp.floor(begin * (1.0 / 16.0))
        send_ref[pl.ds(part * SEG + CAP, META), :] = jnp.where(
            top, high, begin - 16.0 * high
        ).astype(BF16)
    loads[2].wait()
    field[...] = state_ref[...].astype(F32)
    copy.wait()

    def line(i, _):
        for q in range(0, width, GROUP):
            values = [field[pl.ds(i * width + q + j, 1), :] for j in range(GROUP)]
            spots = [code_smem[i, q + j] for j in range(GROUP)]
            for value, at in zip(values, spots):
                packed[pl.ds(at, 1), :] = value
        return 0

    lax.fori_loop(0, rows_here, line, 0)
    for part in range(nparts):
        send_ref[pl.ds(part * SEG, CAP), :] = packed[pl.ds(part * SEG, CAP), :].astype(BF16)
    fetch.wait()


def pack(me, slots, hits, flat, sens, nparts, lines):
    nblocks, width = slots.shape
    cells = flat.shape[0]
    return pl.pallas_call(
        lambda *refs: pack_kernel(nparts, lines, *refs),
        out_shape=(
            jax.ShapeDtypeStruct((nparts * SEG, width), BF16),
            jax.ShapeDtypeStruct((cells // width, width), jnp.int32),
            pltpu.VMEM(sens.shape, BF16),
        ),
        in_specs=[pl.BlockSpec(memory_space=pltpu.SMEM)]
        + [pl.BlockSpec(memory_space=pltpu.HBM)] * 4,
        out_specs=[pl.BlockSpec(memory_space=pltpu.VMEM)] * 3,
        scratch_shapes=[
            pltpu.VMEM((nblocks, width), jnp.int32),
            pltpu.VMEM((nblocks, width), jnp.int32),
            pltpu.VMEM((cells, width), BF16),
            pltpu.VMEM((cells, width), F32),
            pltpu.VMEM((nparts * SEG, width), F32),
            pltpu.VMEM((cells // width, width), jnp.int32),
            pltpu.SMEM((cells // width, width), jnp.int32),
            pltpu.SemaphoreType.DMA((5,)),
        ],
        compiler_params=pltpu.CompilerParams(vmem_limit_bytes=36 << 20),
    )(me, *[pltpu.with_memory_space_constraint(each, pltpu.HBM) for each in (slots, hits, flat, sens)])


def react_kernel(
    nparts, nblocks, entries_ref, recv_ref, value_ref, base_ref, sens_ref, out_ref,
    rows, mapped, table, begin_vmem, begin_smem, next_vmem, next_smem, sems,
):
    width = recv_ref.shape[1]
    depth = base_ref.shape[0]
    for part in range(nparts):
        meta = recv_ref[pl.ds(part * SEG + CAP, META), :].astype(F32)
        begin_vmem[pl.ds(part, 1), :] = (meta[0:1] * 16.0 + meta[1:2]).astype(jnp.int32)
    begin = begin_vmem[...]
    begin_vmem[...] = begin + SEG * iota((nparts, width), 0)
    copy = pltpu.make_async_copy(begin_vmem, begin_smem, sems.at[0])
    copy.start()
    lane = iota((nparts, width), 1)
    counts = pltpu.roll(begin, width - 1, 1) - begin
    end = width - 1
    following = jnp.where((lane < nblocks) & (counts > WIN), lane, end)
    ahead = 1
    while ahead < width:
        moved = pltpu.roll(following, width - ahead, 1)
        following = jnp.minimum(following, jnp.where(lane + ahead < width, moved, end))
        ahead *= 2
    next_vmem[...] = pltpu.roll(following, end, 1)
    chain = pltpu.make_async_copy(next_vmem, next_smem, sems.at[1])
    chain.start()
    table[pl.ds(0, depth), :] = base_ref[...].astype(F32)
    table[pl.ds(depth, depth), :] = value_ref[...].astype(F32)

    def widen(part, _):
        at = pl.multiple_of(part * SEG, 16)
        rows[pl.ds(at, SEG), :] = recv_ref[pl.ds(at, SEG), :].astype(F32)
        return 0

    lax.fori_loop(0, nparts, widen, 0)
    copy.wait()

    def delta(at, entry):
        base = table[pl.ds(entry, 1), :]
        return rows[pl.ds(at, WIN), :] - base

    def batch(part, first):
        at = [begin_smem[part, first + i] for i in range(GROUPS + 1)]
        entry = [entries_ref[0, 0, part * nblocks + first + i] for i in range(GROUPS)]
        dx = [delta(at[i], entry[i]) for i in range(GROUPS)]
        results = []
        for i in range(0, GROUPS, 2):
            product = dot(
                jnp.concatenate([dx[i], dx[i + 1]], axis=0).astype(BF16),
                jnp.concatenate([sens_ref[entry[i]], sens_ref[entry[i + 1]]], axis=1),
            )
            results.append(product[:WIN, :width] + table[pl.ds(entry[i] + depth, 1), :])
            results.append(product[WIN:, width:] + table[pl.ds(entry[i + 1] + depth, 1), :])
        for i in range(GROUPS):
            mapped[pl.ds(at[i], WIN), :] = results[i]

    def sources(step, _):
        for i in range(PARTS):
            batch(step * PARTS + i, 0)
        return 0

    lax.fori_loop(0, nparts // PARTS, sources, 0)

    def rest(part, _):
        def group(k):
            entry = entries_ref[0, 0, part * nblocks + k]
            at, stop = begin_smem[part, k], begin_smem[part, k + 1]

            def more(here):
                result = dot(delta(here, entry).astype(BF16), sens_ref[entry])
                result = result + table[pl.ds(entry + depth, 1), :]
                mapped[pl.ds(here, WIN), :] = jnp.where(
                    iota((WIN, width), 0) < stop - here, result, mapped[pl.ds(here, WIN), :]
                )
                return here + WIN

            lax.while_loop(lambda here: here < stop, more, at + WIN)
            return next_smem[part, k]

        lax.while_loop(lambda k: k < end, group, next_smem[part, end])
        return 0

    chain.wait()
    lax.fori_loop(0, nparts, rest, 0)

    def narrow(part, _):
        out_ref[pl.ds(pl.multiple_of(part * CAP, 16), CAP), :] = mapped[
            pl.ds(pl.multiple_of(part * SEG, 16), CAP), :
        ].astype(BF16)
        return 0

    lax.fori_loop(0, nparts, narrow, 0)


def react(entries, recv, value, base, sens, nparts):
    width = recv.shape[1]
    nblocks = entries.shape[-1] // nparts
    return pl.pallas_call(
        lambda *refs: react_kernel(nparts, nblocks, *refs),
        out_shape=jax.ShapeDtypeStruct((nparts * CAP, width), BF16),
        in_specs=[pl.BlockSpec(memory_space=pltpu.SMEM)]
        + [pl.BlockSpec(memory_space=pltpu.VMEM)] * 4,
        out_specs=pl.BlockSpec(memory_space=pltpu.VMEM),
        scratch_shapes=[
            pltpu.VMEM((nparts * SEG + WIN, width), F32),
            pltpu.VMEM((nparts * SEG + WIN, width), F32),
            pltpu.VMEM((2 * base.shape[0], width), F32),
            pltpu.VMEM((nparts, width), jnp.int32),
            pltpu.SMEM((nparts, width), jnp.int32),
            pltpu.VMEM((nparts, width), jnp.int32),
            pltpu.SMEM((nparts, width), jnp.int32),
            pltpu.SemaphoreType.DMA((2,)),
        ],
        compiler_params=pltpu.CompilerParams(vmem_limit_bytes=24 << 20),
    )(entries, recv, value, base, sens)


def edges_kernel(
    lines, me_ref, code_ref, ret_ref, along1_ref, along2_ref, across1_ref, across2_ref, rows
):
    rows_here, width = code_ref.shape
    cols_here = width
    rows[...] = ret_ref[...].astype(F32)
    along, across = me_ref[0] & 1, (me_ref[0] // lines) & 1

    def gather(out, spots):
        for first in range(0, len(spots), GROUP):
            out[pl.ds(first, GROUP), :] = jnp.concatenate(
                [rows[pl.ds(at, 1), :] for at in spots[first : first + GROUP]], axis=0
            ).astype(BF16)

    for out, line in (
        (along1_ref, (1 - along) * (rows_here - 1)),
        (along2_ref, along * (rows_here - 1)),
    ):
        gather(out, [code_ref[line, j] for j in range(cols_here)])
    for out, column in (
        (across1_ref, (1 - across) * (cols_here - 1)),
        (across2_ref, across * (cols_here - 1)),
    ):
        gather(out, [code_ref[i, column] for i in range(rows_here)])


def edges(me, code, ret, lines):
    rows_here, width = code.shape
    ends = [rows_here if side else width for side in (0, 0, 1, 1)]
    return pl.pallas_call(
        lambda *refs: edges_kernel(lines, *refs),
        out_shape=[jax.ShapeDtypeStruct((end, width), BF16) for end in ends],
        in_specs=[pl.BlockSpec(memory_space=pltpu.SMEM)] * 2
        + [pl.BlockSpec(memory_space=pltpu.VMEM)],
        out_specs=[pl.BlockSpec(memory_space=pltpu.VMEM)] * 4,
        scratch_shapes=[pltpu.VMEM(ret.shape, F32)],
        compiler_params=pltpu.CompilerParams(vmem_limit_bytes=20 << 20),
    )(me, code, ret)


def unpack_kernel(code_ref, ret_ref, out_ref, rows):
    rows_here, width = code_ref.shape
    rows[...] = ret_ref[...].astype(F32)

    def line(i, _):
        for q in range(0, width, GROUP):
            spots = [code_ref[i, q + j] for j in range(GROUP)]
            values = [rows[pl.ds(at, 1), :] for at in spots]
            for j, value in enumerate(values):
                out_ref[pl.ds(i * width + q + j, 1), :] = value
        return 0

    lax.fori_loop(0, rows_here, line, 0)


def unpack(code, ret):
    cells, width = code.size, ret.shape[1]
    return pl.pallas_call(
        unpack_kernel,
        out_shape=jax.ShapeDtypeStruct((cells, width), F32),
        in_specs=[
            pl.BlockSpec(memory_space=pltpu.SMEM),
            pl.BlockSpec(memory_space=pltpu.VMEM),
        ],
        out_specs=pl.BlockSpec(memory_space=pltpu.VMEM),
        scratch_shapes=[pltpu.VMEM(ret.shape, F32)],
        compiler_params=pltpu.CompilerParams(vmem_limit_bytes=20 << 20),
        cost_estimate=pl.CostEstimate(flops=0, bytes_accessed=16 << 20, transcendentals=0),
    )(code, ret)


def transport_kernel(
    nparts, lines, me_ref, mid_ref, along1_ref, along2_ref, across1_ref, across2_ref,
    courant_ref, diffusion_ref, out_hbm, out_ref, sems,
):
    rows_here, cols, width = mid_ref.shape

    def sides(at, count, one, two):
        one, two = one[...].astype(F32), two[...].astype(F32)
        odd = (at & 1) == 1
        before, behind = jnp.where(odd, one, two), jnp.where(odd, two, one)
        return jnp.where(at > 0, before, 0.0), jnp.where(at < count - 1, behind, 0.0)

    across, along = me_ref[0] // lines, me_ref[0] & (lines - 1)
    up, down = sides(along, lines, along1_ref, along2_ref)
    left_side, right_side = sides(across, nparts, across1_ref, across2_ref)
    diffusion = diffusion_ref[...]
    first = iota((cols, width), 0) == 0
    last = iota((cols, width), 0) == cols - 1

    def row(i):
        if i < 0:
            return up
        if i >= rows_here:
            return down
        return mid_ref[i]

    stores = []
    above, here = row(-1), row(0)
    for i in range(rows_here):
        below = row(i + 1)
        left = jnp.where(first, left_side[i : i + 1, :], pltpu.roll(here, 1, 0))
        right = jnp.where(
            last, right_side[i : i + 1, :], pltpu.roll(here, cols - 1, 0)
        )
        courant = courant_ref[:, i : i + 1]
        out_ref[i] = (
            here
            - courant * (here - above)
            + diffusion * (above + below + left + right - 4.0 * here)
        )
        above, here = here, below
        if i % STEP == STEP - 1:
            piece = pl.ds(i + 1 - STEP, STEP)
            stores.append(
                pltpu.make_async_copy(out_ref.at[piece], out_hbm.at[piece], sems.at[i // STEP])
            )
            stores[-1].start()
    for store in stores:
        store.wait()


def transport(me, nparts, lines, reacted, halo, courant, diffusion):
    shape = reacted.shape
    return pl.pallas_call(
        lambda *refs: transport_kernel(nparts, lines, *refs),
        out_shape=jax.ShapeDtypeStruct(shape, F32),
        in_specs=[pl.BlockSpec(memory_space=pltpu.SMEM)]
        + [pl.BlockSpec(memory_space=pltpu.VMEM)] * 7,
        out_specs=pl.BlockSpec(memory_space=pl.ANY),
        scratch_shapes=[
            pltpu.VMEM(shape, F32),
            pltpu.SemaphoreType.DMA((shape[0] // STEP,)),
        ],
        compiler_params=pltpu.CompilerParams(vmem_limit_bytes=20 << 20),
    )(me, reacted, *halo, courant, diffusion)


def swapped(block, axis, first):
    count = lax.axis_size(axis)
    pairs = [(i, (i + 1) % count) for i in range(first, count, 2)]
    return lax.ppermute(block, axis, pairs + [(j, i) for i, j in pairs])


def local(
    state, courant, diffusion, table_value, table_base, table_sens, slot_cell, hit_step, entry_ids
):
    rows_here, cols_here, width = state.shape
    cells = rows_here * cols_here
    nparts, lines = lax.axis_size("blk"), lax.axis_size("grid")
    me = lax.axis_index(("blk", "grid")).astype(jnp.int32).reshape(1)
    flat = state.reshape(cells, width)
    send, code, sens = pack(me, slot_cell[0], hit_step[0], flat, table_sens, nparts, lines)
    recv = lax.all_to_all(send.reshape(nparts, SEG, width), "blk", 0, 0, tiled=True)
    done = react(
        entry_ids, recv.reshape(nparts * SEG, width),
        table_value, table_base, sens, nparts,
    )
    back = lax.all_to_all(done.reshape(nparts, CAP, width), "blk", 0, 0, tiled=True)
    back = back.reshape(nparts * CAP, width)
    along1, along2, across1, across2 = edges(me, code, back, lines)
    halo = (
        swapped(along1, "grid", 0), swapped(along2, "grid", 1),
        swapped(across1, "blk", 0), swapped(across2, "blk", 1),
    )
    reacted = unpack(code, back).reshape(rows_here, cols_here, width)
    return transport(me, nparts, lines, reacted, halo, courant.T, diffusion.reshape(1, width))


def solution(mesh):
    return jax.shard_map(
        local,
        mesh=mesh,
        in_specs=(
            P("grid", "blk", None),
            P("grid", "blk"),
            P(),
            P("blk", None),
            P("blk", None),
            P("blk", None, None),
            P("grid", "blk", None),
            P("grid", "blk", None),
            P("blk", "grid", None),
        ),
        out_specs=P("grid", "blk", None),
        check_vma=False,
    )
```

```python
import jax
import jax.numpy as jnp
from jax import lax
from jax.experimental import pallas as pl
from jax.experimental.pallas import tpu as pltpu
from jax.sharding import PartitionSpec as P

F32 = jnp.float32
BF16 = jnp.bfloat16
CAP = 512
META = 16
SEG = CAP + META
WIN = 24
GROUPS = 48
STEP = 4
PARTS = 8
GROUP = 16


def iota(shape, dim):
    return lax.broadcasted_iota(jnp.int32, shape, dim)


def zero_one(mask):
    return jnp.where(mask, 1.0, 0.0).astype(BF16)


def dot(a, b):
    return lax.dot_general(a, b, (((1,), (0,)), ((), ())), preferred_element_type=F32)


def dot_nt(a, b):
    return lax.dot_general(a, b, (((1,), (1,)), ((), ())), preferred_element_type=F32)


def pack_kernel(
    nparts, lines, me_ref, slots_hbm, hits_hbm, state_hbm, sens_hbm, send_ref, back_ref, sens_ref,
    slots_ref, hits_ref, state_ref, field, packed, code_vmem, code_smem, sems,
):
    nblocks, width = slots_ref.shape
    cells = state_ref.shape[0]
    rows_here = cells // width
    loads = [
        pltpu.make_async_copy(slots_hbm, slots_ref, sems.at[0]),
        pltpu.make_async_copy(hits_hbm, hits_ref, sems.at[1]),
        pltpu.make_async_copy(state_hbm, state_ref, sems.at[2]),
    ]
    for load in loads:
        load.start()
    fetch = pltpu.make_async_copy(sens_hbm, sens_ref, sems.at[4])
    fetch.start()
    before = zero_one(iota((width, width), 0) < iota((width, width), 1))
    weights = jnp.concatenate([jnp.ones((width, width), BF16), before], axis=0)
    earlier = zero_one(iota((nblocks, nblocks), 1) < iota((nblocks, nblocks), 0))
    starts = zero_one(iota((nblocks, width), 0) < iota((nblocks, width), 1))
    ones = jnp.ones((META, width), BF16)
    top = iota((META, width), 0) == 0
    loads[0].wait()
    loads[1].wait()
    slots = slots_ref[...]
    live = slots >= 0
    owner = jnp.where(live, (hits_ref[...] + (me_ref[0] // lines)) & (nparts - 1), nparts)
    mine = [owner == part for part in range(nparts)]
    masks = [zero_one(each) for each in mine]
    ahead = [dot(earlier, mask).astype(BF16) for mask in masks]
    ranks = dot(
        jnp.concatenate(
            [jnp.concatenate([a, m], axis=1) for a, m in zip(ahead, masks)], axis=0
        ),
        weights,
    )
    place = jnp.zeros((nblocks, width), F32)
    for part in range(nparts):
        place = place + jnp.where(mine[part], ranks[part * nblocks : (part + 1) * nblocks], 0.0)
    spot = owner * CAP + place.astype(jnp.int32)
    spot_high = (spot >> 7).astype(F32)
    spot_low = (spot & 127).astype(F32)
    cell_row = slots >> 7
    cell_col = slots & 127
    total = jnp.zeros((2 * rows_here, width), F32)
    row_ids = iota((rows_here, width), 0)
    col_ids = iota((width, width), 0)
    for pair in range(0, nblocks, 2):
        lhs, rhs = [], []
        for k in (pair, pair + 1):
            at_row = row_ids == cell_row[k : k + 1, :]
            lhs.append(
                jnp.concatenate(
                    [
                        jnp.where(at_row, spot_high[k : k + 1, :], 0.0),
                        jnp.where(at_row, spot_low[k : k + 1, :], 0.0),
                    ],
                    axis=0,
                ).astype(BF16)
            )
            rhs.append(zero_one(col_ids == cell_col[k : k + 1, :]))
        total = total + dot_nt(jnp.concatenate(lhs, axis=1), jnp.concatenate(rhs, axis=1))
    back = (total[:rows_here] * 128.0 + total[rows_here:]).astype(jnp.int32)
    back_ref[...] = back
    code_vmem[...] = back + (back >> 9) * META
    copy = pltpu.make_async_copy(code_vmem, code_smem, sems.at[3])
    copy.start()
    counts = jnp.concatenate([dot_nt(ones, mask) for mask in masks], axis=0).astype(BF16)
    begins = dot(counts, starts)
    for part in range(nparts):
        begin = begins[part * META : (part + 1) * META]
        high = jnp.floor(begin * (1.0 / 16.0))
        send_ref[pl.ds(part * SEG + CAP, META), :] = jnp.where(
            top, high, begin - 16.0 * high
        ).astype(BF16)
    loads[2].wait()
    field[...] = state_ref[...].astype(F32)
    copy.wait()

    def line(i, _):
        for q in range(0, width, GROUP):
            values = [field[pl.ds(i * width + q + j, 1), :] for j in range(GROUP)]
            spots = [code_smem[i, q + j] for j in range(GROUP)]
            for value, at in zip(values, spots):
                packed[pl.ds(at, 1), :] = value
        return 0

    lax.fori_loop(0, rows_here, line, 0, unroll=2)
    for part in range(nparts):
        send_ref[pl.ds(part * SEG, CAP), :] = packed[pl.ds(part * SEG, CAP), :].astype(BF16)
    fetch.wait()


def pack(me, slots, hits, flat, sens, nparts, lines):
    nblocks, width = slots.shape
    cells = flat.shape[0]
    return pl.pallas_call(
        lambda *refs: pack_kernel(nparts, lines, *refs),
        out_shape=(
            jax.ShapeDtypeStruct((nparts * SEG, width), BF16),
            jax.ShapeDtypeStruct((cells // width, width), jnp.int32),
            pltpu.VMEM(sens.shape, BF16),
        ),
        in_specs=[pl.BlockSpec(memory_space=pltpu.SMEM)]
        + [pl.BlockSpec(memory_space=pltpu.HBM)] * 4,
        out_specs=[pl.BlockSpec(memory_space=pltpu.VMEM)] * 3,
        scratch_shapes=[
            pltpu.VMEM((nblocks, width), jnp.int32),
            pltpu.VMEM((nblocks, width), jnp.int32),
            pltpu.VMEM((cells, width), BF16),
            pltpu.VMEM((cells, width), F32),
            pltpu.VMEM((nparts * SEG, width), F32),
            pltpu.VMEM((cells // width, width), jnp.int32),
            pltpu.SMEM((cells // width, width), jnp.int32),
            pltpu.SemaphoreType.DMA((5,)),
        ],
        compiler_params=pltpu.CompilerParams(vmem_limit_bytes=36 << 20),
    )(me, *[pltpu.with_memory_space_constraint(each, pltpu.HBM) for each in (slots, hits, flat, sens)])


def react_kernel(
    nparts, nblocks, entries_ref, recv_ref, value_ref, base_ref, sens_ref, out_ref,
    rows, mapped, table, begin_vmem, begin_smem, next_vmem, next_smem, sems,
):
    width = recv_ref.shape[1]
    depth = base_ref.shape[0]
    for part in range(nparts):
        meta = recv_ref[pl.ds(part * SEG + CAP, META), :].astype(F32)
        begin_vmem[pl.ds(part, 1), :] = (meta[0:1] * 16.0 + meta[1:2]).astype(jnp.int32)
    begin = begin_vmem[...]
    begin_vmem[...] = begin + SEG * iota((nparts, width), 0)
    copy = pltpu.make_async_copy(begin_vmem, begin_smem, sems.at[0])
    copy.start()
    lane = iota((nparts, width), 1)
    counts = pltpu.roll(begin, width - 1, 1) - begin
    end = width - 1
    following = jnp.where((lane < nblocks) & (counts > WIN), lane, end)
    ahead = 1
    while ahead < width:
        moved = pltpu.roll(following, width - ahead, 1)
        following = jnp.minimum(following, jnp.where(lane + ahead < width, moved, end))
        ahead *= 2
    next_vmem[...] = pltpu.roll(following, end, 1)
    chain = pltpu.make_async_copy(next_vmem, next_smem, sems.at[1])
    chain.start()
    table[:, 0:1, :] = base_ref[...].astype(F32).reshape(depth, 1, width)
    table[:, 1:2, :] = value_ref[...].astype(F32).reshape(depth, 1, width)

    def widen(part, _):
        at = pl.multiple_of(part * SEG, 16)
        rows[pl.ds(at, SEG), :] = recv_ref[pl.ds(at, SEG), :].astype(F32)
        return 0

    lax.fori_loop(0, nparts, widen, 0)
    copy.wait()

    def delta(at, entry):
        base = table[entry, 0:1, :]
        return rows[pl.ds(at, WIN), :] - base

    def batch(part, first):
        at = [begin_smem[part, first + i] for i in range(GROUPS + 1)]
        entry = [entries_ref[0, 0, part * nblocks + first + i] for i in range(GROUPS)]
        dx = [delta(at[i], entry[i]) for i in range(GROUPS)]
        results = []
        for i in range(0, GROUPS, 2):
            product = dot(
                jnp.concatenate([dx[i], dx[i + 1]], axis=0).astype(BF16),
                jnp.concatenate([sens_ref[entry[i]], sens_ref[entry[i + 1]]], axis=1),
            )
            results.append(product[:WIN, :width] + table[entry[i], 1:2, :])
            results.append(product[WIN:, width:] + table[entry[i + 1], 1:2, :])
        for i in range(GROUPS):
            mapped[pl.ds(at[i], WIN), :] = results[i]

    def sources(step, _):
        for i in range(PARTS):
            batch(step * PARTS + i, 0)
        return 0

    lax.fori_loop(0, nparts // PARTS, sources, 0)

    def rest(part, _):
        def group(k):
            entry = entries_ref[0, 0, part * nblocks + k]
            at, stop = begin_smem[part, k], begin_smem[part, k + 1]

            def more(here):
                result = dot(delta(here, entry).astype(BF16), sens_ref[entry])
                result = result + table[entry, 1:2, :]
                mapped[pl.ds(here, WIN), :] = jnp.where(
                    iota((WIN, width), 0) < stop - here, result, mapped[pl.ds(here, WIN), :]
                )
                return here + WIN

            lax.while_loop(lambda here: here < stop, more, at + WIN)
            return next_smem[part, k]

        lax.while_loop(lambda k: k < end, group, next_smem[part, end])
        return 0

    chain.wait()
    lax.fori_loop(0, nparts, rest, 0)

    def narrow(part, _):
        out_ref[pl.ds(pl.multiple_of(part * CAP, 16), CAP), :] = mapped[
            pl.ds(pl.multiple_of(part * SEG, 16), CAP), :
        ].astype(BF16)
        return 0

    lax.fori_loop(0, nparts, narrow, 0)


def react(entries, recv, value, base, sens, nparts):
    width = recv.shape[1]
    nblocks = entries.shape[-1] // nparts
    return pl.pallas_call(
        lambda *refs: react_kernel(nparts, nblocks, *refs),
        out_shape=jax.ShapeDtypeStruct((nparts * CAP, width), BF16),
        in_specs=[pl.BlockSpec(memory_space=pltpu.SMEM)]
        + [pl.BlockSpec(memory_space=pltpu.VMEM)] * 4,
        out_specs=pl.BlockSpec(memory_space=pltpu.VMEM),
        scratch_shapes=[
            pltpu.VMEM((nparts * SEG + WIN, width), F32),
            pltpu.VMEM((nparts * SEG + WIN, width), F32),
            pltpu.VMEM((base.shape[0], 8, width), F32),
            pltpu.VMEM((nparts, width), jnp.int32),
            pltpu.SMEM((nparts, width), jnp.int32),
            pltpu.VMEM((nparts, width), jnp.int32),
            pltpu.SMEM((nparts, width), jnp.int32),
            pltpu.SemaphoreType.DMA((2,)),
        ],
        compiler_params=pltpu.CompilerParams(vmem_limit_bytes=24 << 20),
    )(entries, recv, value, base, sens)


def edges_kernel(
    lines, me_ref, code_ref, ret_ref, along1_ref, along2_ref, across1_ref, across2_ref, rows
):
    rows_here, width = code_ref.shape
    cols_here = width
    rows[...] = ret_ref[...].astype(F32)
    along, across = me_ref[0] & 1, (me_ref[0] // lines) & 1

    def gather(out, spots):
        for first in range(0, len(spots), GROUP):
            out[pl.ds(first, GROUP), :] = jnp.concatenate(
                [rows[pl.ds(at, 1), :] for at in spots[first : first + GROUP]], axis=0
            ).astype(BF16)

    for out, line in (
        (along1_ref, (1 - along) * (rows_here - 1)),
        (along2_ref, along * (rows_here - 1)),
    ):
        gather(out, [code_ref[line, j] for j in range(cols_here)])
    for out, column in (
        (across1_ref, (1 - across) * (cols_here - 1)),
        (across2_ref, across * (cols_here - 1)),
    ):
        gather(out, [code_ref[i, column] for i in range(rows_here)])


def edges(me, code, ret, lines):
    rows_here, width = code.shape
    ends = [rows_here if side else width for side in (0, 0, 1, 1)]
    return pl.pallas_call(
        lambda *refs: edges_kernel(lines, *refs),
        out_shape=[jax.ShapeDtypeStruct((end, width), BF16) for end in ends],
        in_specs=[pl.BlockSpec(memory_space=pltpu.SMEM)] * 2
        + [pl.BlockSpec(memory_space=pltpu.VMEM)],
        out_specs=[pl.BlockSpec(memory_space=pltpu.VMEM)] * 4,
        scratch_shapes=[pltpu.VMEM(ret.shape, F32)],
        compiler_params=pltpu.CompilerParams(vmem_limit_bytes=20 << 20),
    )(me, code, ret)


def unpack_kernel(code_ref, ret_ref, out_ref, rows):
    rows_here, width = code_ref.shape
    rows[...] = ret_ref[...].astype(F32)

    def line(i, _):
        for q in range(0, width, GROUP):
            spots = [code_ref[i, q + j] for j in range(GROUP)]
            values = [rows[pl.ds(at, 1), :] for at in spots]
            for j, value in enumerate(values):
                out_ref[pl.ds(i * width + q + j, 1), :] = value
        return 0

    lax.fori_loop(0, rows_here, line, 0, unroll=2)


def unpack(code, ret):
    cells, width = code.size, ret.shape[1]
    return pl.pallas_call(
        unpack_kernel,
        out_shape=jax.ShapeDtypeStruct((cells, width), F32),
        in_specs=[
            pl.BlockSpec(memory_space=pltpu.SMEM),
            pl.BlockSpec(memory_space=pltpu.VMEM),
        ],
        out_specs=pl.BlockSpec(memory_space=pltpu.VMEM),
        scratch_shapes=[pltpu.VMEM(ret.shape, F32)],
        compiler_params=pltpu.CompilerParams(vmem_limit_bytes=20 << 20),
        cost_estimate=pl.CostEstimate(flops=0, bytes_accessed=16 << 20, transcendentals=0),
    )(code, ret)


def transport_kernel(
    nparts, lines, me_ref, mid_ref, along1_ref, along2_ref, across1_ref, across2_ref,
    courant_ref, diffusion_ref, out_hbm, out_ref, sems,
):
    rows_here, cols, width = mid_ref.shape

    def sides(at, count, one, two):
        one, two = one[...].astype(F32), two[...].astype(F32)
        odd = (at & 1) == 1
        before, behind = jnp.where(odd, one, two), jnp.where(odd, two, one)
        return jnp.where(at > 0, before, 0.0), jnp.where(at < count - 1, behind, 0.0)

    across, along = me_ref[0] // lines, me_ref[0] & (lines - 1)
    up, down = sides(along, lines, along1_ref, along2_ref)
    left_side, right_side = sides(across, nparts, across1_ref, across2_ref)
    diffusion = diffusion_ref[...]
    first = iota((cols, width), 0) == 0
    last = iota((cols, width), 0) == cols - 1

    def row(i):
        if i < 0:
            return up
        if i >= rows_here:
            return down
        return mid_ref[i]

    stores = []
    above, here = row(-1), row(0)
    for i in range(rows_here):
        below = row(i + 1)
        left = jnp.where(first, left_side[i : i + 1, :], pltpu.roll(here, 1, 0))
        right = jnp.where(
            last, right_side[i : i + 1, :], pltpu.roll(here, cols - 1, 0)
        )
        courant = courant_ref[:, i : i + 1]
        out_ref[i] = (
            here
            - courant * (here - above)
            + diffusion * (above + below + left + right - 4.0 * here)
        )
        above, here = here, below
        if i % STEP == STEP - 1:
            piece = pl.ds(i + 1 - STEP, STEP)
            stores.append(
                pltpu.make_async_copy(out_ref.at[piece], out_hbm.at[piece], sems.at[i // STEP])
            )
            stores[-1].start()
    for store in stores:
        store.wait()


def transport(me, nparts, lines, reacted, halo, courant, diffusion):
    shape = reacted.shape
    return pl.pallas_call(
        lambda *refs: transport_kernel(nparts, lines, *refs),
        out_shape=jax.ShapeDtypeStruct(shape, F32),
        in_specs=[pl.BlockSpec(memory_space=pltpu.SMEM)]
        + [pl.BlockSpec(memory_space=pltpu.VMEM)] * 7,
        out_specs=pl.BlockSpec(memory_space=pl.ANY),
        scratch_shapes=[
            pltpu.VMEM(shape, F32),
            pltpu.SemaphoreType.DMA((shape[0] // STEP,)),
        ],
        compiler_params=pltpu.CompilerParams(vmem_limit_bytes=20 << 20),
    )(me, reacted, *halo, courant, diffusion)


def swapped(block, axis, first):
    count = lax.axis_size(axis)
    pairs = [(i, (i + 1) % count) for i in range(first, count, 2)]
    return lax.ppermute(block, axis, pairs + [(j, i) for i, j in pairs])


def local(
    state, courant, diffusion, table_value, table_base, table_sens, slot_cell, hit_step, entry_ids
):
    rows_here, cols_here, width = state.shape
    cells = rows_here * cols_here
    nparts, lines = lax.axis_size("blk"), lax.axis_size("grid")
    me = lax.axis_index(("blk", "grid")).astype(jnp.int32).reshape(1)
    flat = state.reshape(cells, width)
    send, code, sens = pack(me, slot_cell[0], hit_step[0], flat, table_sens, nparts, lines)
    recv = lax.all_to_all(send.reshape(nparts, SEG, width), "blk", 0, 0, tiled=True)
    done = react(
        entry_ids, recv.reshape(nparts * SEG, width),
        table_value, table_base, sens, nparts,
    )
    back = lax.all_to_all(done.reshape(nparts, CAP, width), "blk", 0, 0, tiled=True)
    back = back.reshape(nparts * CAP, width)
    along1, along2, across1, across2 = edges(me, code, back, lines)
    halo = (
        swapped(along1, "grid", 0), swapped(along2, "grid", 1),
        swapped(across1, "blk", 0), swapped(across2, "blk", 1),
    )
    reacted = unpack(code, back).reshape(rows_here, cols_here, width)
    return transport(me, nparts, lines, reacted, halo, courant.T, diffusion.reshape(1, width))


def solution(mesh):
    return jax.shard_map(
        local,
        mesh=mesh,
        in_specs=(
            P("grid", "blk", None),
            P("grid", "blk"),
            P(),
            P("blk", None),
            P("blk", None),
            P("blk", None, None),
            P("grid", "blk", None),
            P("grid", "blk", None),
            P("blk", "grid", None),
        ),
        out_specs=P("grid", "blk", None),
        check_vma=False,
    )
```

```python
import jax
import jax.numpy as jnp
from jax import lax
from jax.experimental import pallas as pl
from jax.experimental.pallas import tpu as pltpu
from jax.sharding import PartitionSpec as P

F32 = jnp.float32
BF16 = jnp.bfloat16
CAP = 512
META = 16
SEG = CAP + META
WIN = 24
GROUPS = 48
STEP = 4
PARTS = 8
GROUP = 16


def iota(shape, dim):
    return lax.broadcasted_iota(jnp.int32, shape, dim)


def zero_one(mask):
    return jnp.where(mask, 1.0, 0.0).astype(BF16)


def dot(a, b):
    return lax.dot_general(a, b, (((1,), (0,)), ((), ())), preferred_element_type=F32)


def dot_nt(a, b):
    return lax.dot_general(a, b, (((1,), (1,)), ((), ())), preferred_element_type=F32)


def pack_kernel(
    nparts, lines, me_ref, slots_hbm, hits_hbm, state_hbm, sens_hbm, send_ref, back_ref, sens_ref,
    slots_ref, hits_ref, state_ref, field, packed, code_vmem, code_smem, sems,
):
    nblocks, width = slots_ref.shape
    cells = state_ref.shape[0]
    rows_here = cells // width
    loads = [
        pltpu.make_async_copy(slots_hbm, slots_ref, sems.at[0]),
        pltpu.make_async_copy(hits_hbm, hits_ref, sems.at[1]),
        pltpu.make_async_copy(state_hbm, state_ref, sems.at[2]),
    ]
    for load in loads:
        load.start()
    fetch = pltpu.make_async_copy(sens_hbm, sens_ref, sems.at[4])
    fetch.start()
    before = zero_one(iota((width, width), 0) < iota((width, width), 1))
    weights = jnp.concatenate([jnp.ones((width, width), BF16), before], axis=0)
    earlier = zero_one(iota((nblocks, nblocks), 1) < iota((nblocks, nblocks), 0))
    starts = zero_one(iota((nblocks, width), 0) < iota((nblocks, width), 1))
    ones = jnp.ones((META, width), BF16)
    top = iota((META, width), 0) == 0
    loads[0].wait()
    loads[1].wait()
    slots = slots_ref[...]
    live = slots >= 0
    owner = jnp.where(live, (hits_ref[...] + (me_ref[0] // lines)) & (nparts - 1), nparts)
    mine = [owner == part for part in range(nparts)]
    masks = [zero_one(each) for each in mine]
    ahead = [dot(earlier, mask).astype(BF16) for mask in masks]
    ranks = dot(
        jnp.concatenate(
            [jnp.concatenate([a, m], axis=1) for a, m in zip(ahead, masks)], axis=0
        ),
        weights,
    )
    place = jnp.zeros((nblocks, width), F32)
    for part in range(nparts):
        place = place + jnp.where(mine[part], ranks[part * nblocks : (part + 1) * nblocks], 0.0)
    spot = owner * CAP + place.astype(jnp.int32)
    spot_high = (spot >> 7).astype(F32)
    spot_low = (spot & 127).astype(F32)
    cell_row = slots >> 7
    cell_col = slots & 127
    total = jnp.zeros((2 * rows_here, width), F32)
    row_ids = iota((rows_here, width), 0)
    col_ids = iota((width, width), 0)
    for pair in range(0, nblocks, 2):
        lhs, rhs = [], []
        for k in (pair, pair + 1):
            at_row = row_ids == cell_row[k : k + 1, :]
            lhs.append(
                jnp.concatenate(
                    [
                        jnp.where(at_row, spot_high[k : k + 1, :], 0.0),
                        jnp.where(at_row, spot_low[k : k + 1, :], 0.0),
                    ],
                    axis=0,
                ).astype(BF16)
            )
            rhs.append(zero_one(col_ids == cell_col[k : k + 1, :]))
        total = total + dot_nt(jnp.concatenate(lhs, axis=1), jnp.concatenate(rhs, axis=1))
    back = (total[:rows_here] * 128.0 + total[rows_here:]).astype(jnp.int32)
    back_ref[...] = back
    code_vmem[...] = back + (back >> 9) * META
    copy = pltpu.make_async_copy(code_vmem, code_smem, sems.at[3])
    copy.start()
    counts = jnp.concatenate([dot_nt(ones, mask) for mask in masks], axis=0).astype(BF16)
    begins = dot(counts, starts)
    for part in range(nparts):
        begin = begins[part * META : (part + 1) * META]
        high = jnp.floor(begin * (1.0 / 16.0))
        send_ref[pl.ds(part * SEG + CAP, META), :] = jnp.where(
            top, high, begin - 16.0 * high
        ).astype(BF16)
    loads[2].wait()
    field[...] = state_ref[...].astype(F32)
    copy.wait()

    def line(i, _):
        for q in range(0, width, GROUP):
            values = [field[pl.ds(i * width + q + j, 1), :] for j in range(GROUP)]
            spots = [code_smem[i, q + j] for j in range(GROUP)]
            for value, at in zip(values, spots):
                packed[pl.ds(at, 1), :] = value
        return 0

    lax.fori_loop(0, rows_here, line, 0, unroll=2)
    for part in range(nparts):
        send_ref[pl.ds(part * SEG, CAP), :] = packed[pl.ds(part * SEG, CAP), :].astype(BF16)
    fetch.wait()


def pack(me, slots, hits, flat, sens, nparts, lines):
    nblocks, width = slots.shape
    cells = flat.shape[0]
    return pl.pallas_call(
        lambda *refs: pack_kernel(nparts, lines, *refs),
        out_shape=(
            jax.ShapeDtypeStruct((nparts * SEG, width), BF16),
            jax.ShapeDtypeStruct((cells // width, width), jnp.int32),
            pltpu.VMEM(sens.shape, BF16),
        ),
        in_specs=[pl.BlockSpec(memory_space=pltpu.SMEM)]
        + [pl.BlockSpec(memory_space=pltpu.HBM)] * 4,
        out_specs=[pl.BlockSpec(memory_space=pltpu.VMEM)] * 3,
        scratch_shapes=[
            pltpu.VMEM((nblocks, width), jnp.int32),
            pltpu.VMEM((nblocks, width), jnp.int32),
            pltpu.VMEM((cells, width), BF16),
            pltpu.VMEM((cells, width), F32),
            pltpu.VMEM((nparts * SEG, width), F32),
            pltpu.VMEM((cells // width, width), jnp.int32),
            pltpu.SMEM((cells // width, width), jnp.int32),
            pltpu.SemaphoreType.DMA((5,)),
        ],
        compiler_params=pltpu.CompilerParams(vmem_limit_bytes=36 << 20),
    )(me, *[pltpu.with_memory_space_constraint(each, pltpu.HBM) for each in (slots, hits, flat, sens)])


def react_kernel(
    nparts, nblocks, entries_ref, recv_ref, value_ref, base_ref, sens_ref, out_ref,
    rows, mapped, table, begin_vmem, begin_smem, next_vmem, next_smem, sems,
):
    width = recv_ref.shape[1]
    depth = base_ref.shape[0]
    for part in range(nparts):
        meta = recv_ref[pl.ds(part * SEG + CAP, META), :].astype(F32)
        begin_vmem[pl.ds(part, 1), :] = (meta[0:1] * 16.0 + meta[1:2]).astype(jnp.int32)
    begin = begin_vmem[...]
    begin_vmem[...] = begin + SEG * iota((nparts, width), 0)
    copy = pltpu.make_async_copy(begin_vmem, begin_smem, sems.at[0])
    copy.start()
    lane = iota((nparts, width), 1)
    counts = pltpu.roll(begin, width - 1, 1) - begin
    end = width - 1
    following = jnp.where((lane < nblocks) & (counts > WIN), lane, end)
    ahead = 1
    while ahead < width:
        moved = pltpu.roll(following, width - ahead, 1)
        following = jnp.minimum(following, jnp.where(lane + ahead < width, moved, end))
        ahead *= 2
    next_vmem[...] = pltpu.roll(following, end, 1)
    chain = pltpu.make_async_copy(next_vmem, next_smem, sems.at[1])
    chain.start()
    table[:, 0:1, :] = base_ref[...].astype(F32).reshape(depth, 1, width)
    table[:, 1:2, :] = value_ref[...].astype(F32).reshape(depth, 1, width)

    def widen(part, _):
        at = pl.multiple_of(part * SEG, 16)
        rows[pl.ds(at, SEG), :] = recv_ref[pl.ds(at, SEG), :].astype(F32)
        return 0

    lax.fori_loop(0, nparts, widen, 0)
    copy.wait()

    def delta(at, entry):
        base = table[entry, 0:1, :]
        return rows[pl.ds(at, WIN), :] - base

    def batch(part, first):
        at = [begin_smem[part, first + i] for i in range(GROUPS + 1)]
        entry = [entries_ref[0, 0, part * nblocks + first + i] for i in range(GROUPS)]
        dx = [delta(at[i], entry[i]) for i in range(GROUPS)]
        results = []
        for i in range(0, GROUPS, 2):
            product = dot(
                jnp.concatenate([dx[i], dx[i + 1]], axis=0).astype(BF16),
                jnp.concatenate([sens_ref[entry[i]], sens_ref[entry[i + 1]]], axis=1),
            )
            results.append(product[:WIN, :width] + table[entry[i], 1:2, :])
            results.append(product[WIN:, width:] + table[entry[i + 1], 1:2, :])
        for i in range(GROUPS):
            mapped[pl.ds(at[i], WIN), :] = results[i]

    def sources(step, _):
        for i in range(PARTS):
            batch(step * PARTS + i, 0)
        return 0

    lax.fori_loop(0, nparts // PARTS, sources, 0)

    def rest(part, _):
        def group(k):
            entry = entries_ref[0, 0, part * nblocks + k]
            at, stop = begin_smem[part, k], begin_smem[part, k + 1]

            def more(here):
                result = dot(delta(here, entry).astype(BF16), sens_ref[entry])
                result = result + table[entry, 1:2, :]
                mapped[pl.ds(here, WIN), :] = jnp.where(
                    iota((WIN, width), 0) < stop - here, result, mapped[pl.ds(here, WIN), :]
                )
                return here + WIN

            lax.while_loop(lambda here: here < stop, more, at + WIN)
            return next_smem[part, k]

        lax.while_loop(lambda k: k < end, group, next_smem[part, end])
        return 0

    chain.wait()
    lax.fori_loop(0, nparts, rest, 0)

    def narrow(part, _):
        out_ref[pl.ds(pl.multiple_of(part * CAP, 16), CAP), :] = mapped[
            pl.ds(pl.multiple_of(part * SEG, 16), CAP), :
        ].astype(BF16)
        return 0

    lax.fori_loop(0, nparts, narrow, 0)


def react(entries, recv, value, base, sens, nparts):
    width = recv.shape[1]
    nblocks = entries.shape[-1] // nparts
    return pl.pallas_call(
        lambda *refs: react_kernel(nparts, nblocks, *refs),
        out_shape=jax.ShapeDtypeStruct((nparts * CAP, width), BF16),
        in_specs=[pl.BlockSpec(memory_space=pltpu.SMEM)]
        + [pl.BlockSpec(memory_space=pltpu.VMEM)] * 4,
        out_specs=pl.BlockSpec(memory_space=pltpu.VMEM),
        scratch_shapes=[
            pltpu.VMEM((nparts * SEG + WIN, width), F32),
            pltpu.VMEM((nparts * SEG + WIN, width), F32),
            pltpu.VMEM((base.shape[0], 8, width), F32),
            pltpu.VMEM((nparts, width), jnp.int32),
            pltpu.SMEM((nparts, width), jnp.int32),
            pltpu.VMEM((nparts, width), jnp.int32),
            pltpu.SMEM((nparts, width), jnp.int32),
            pltpu.SemaphoreType.DMA((2,)),
        ],
        compiler_params=pltpu.CompilerParams(vmem_limit_bytes=24 << 20),
    )(entries, recv, value, base, sens)


def edges_kernel(
    lines, me_ref, code_ref, ret_ref, along1_ref, along2_ref, across1_ref, across2_ref, rows
):
    rows_here, width = code_ref.shape
    cols_here = width
    rows[...] = ret_ref[...].astype(F32)
    along, across = me_ref[0] & 1, (me_ref[0] // lines) & 1

    def gather(out, spots):
        for first in range(0, len(spots), GROUP):
            out[pl.ds(first, GROUP), :] = jnp.concatenate(
                [rows[pl.ds(at, 1), :] for at in spots[first : first + GROUP]], axis=0
            ).astype(BF16)

    for out, line in (
        (along1_ref, (1 - along) * (rows_here - 1)),
        (along2_ref, along * (rows_here - 1)),
    ):
        gather(out, [code_ref[line, j] for j in range(cols_here)])
    for out, column in (
        (across1_ref, (1 - across) * (cols_here - 1)),
        (across2_ref, across * (cols_here - 1)),
    ):
        gather(out, [code_ref[i, column] for i in range(rows_here)])


def edges(me, code, ret, lines):
    rows_here, width = code.shape
    ends = [rows_here if side else width for side in (0, 0, 1, 1)]
    return pl.pallas_call(
        lambda *refs: edges_kernel(lines, *refs),
        out_shape=[jax.ShapeDtypeStruct((end, width), BF16) for end in ends],
        in_specs=[pl.BlockSpec(memory_space=pltpu.SMEM)] * 2
        + [pl.BlockSpec(memory_space=pltpu.VMEM)],
        out_specs=[pl.BlockSpec(memory_space=pltpu.VMEM)] * 4,
        scratch_shapes=[pltpu.VMEM(ret.shape, F32)],
        compiler_params=pltpu.CompilerParams(vmem_limit_bytes=20 << 20),
    )(me, code, ret)


def unpack_kernel(code_ref, ret_ref, out_ref, rows):
    rows_here, width = code_ref.shape
    rows[...] = ret_ref[...].astype(F32)

    def line(i, _):
        for q in range(0, width, GROUP):
            spots = [code_ref[i, q + j] for j in range(GROUP)]
            values = [rows[pl.ds(at, 1), :] for at in spots]
            for j, value in enumerate(values):
                out_ref[pl.ds(i * width + q + j, 1), :] = value
        return 0

    lax.fori_loop(0, rows_here, line, 0, unroll=2)


def unpack(code, ret):
    cells, width = code.size, ret.shape[1]
    return pl.pallas_call(
        unpack_kernel,
        out_shape=jax.ShapeDtypeStruct((cells, width), F32),
        in_specs=[
            pl.BlockSpec(memory_space=pltpu.SMEM),
            pl.BlockSpec(memory_space=pltpu.VMEM),
        ],
        out_specs=pl.BlockSpec(memory_space=pltpu.VMEM),
        scratch_shapes=[pltpu.VMEM(ret.shape, F32)],
        compiler_params=pltpu.CompilerParams(vmem_limit_bytes=20 << 20),
        cost_estimate=pl.CostEstimate(flops=0, bytes_accessed=16 << 20, transcendentals=0),
    )(code, ret)


def transport_kernel(
    nparts, lines, me_ref, mid_ref, along1_ref, along2_ref, across1_ref, across2_ref,
    courant_ref, diffusion_ref, out_hbm, out_ref, sems,
):
    rows_here, cols, width = out_ref.shape

    def sides(at, count, one, two):
        one, two = one[...].astype(F32), two[...].astype(F32)
        odd = (at & 1) == 1
        before, behind = jnp.where(odd, one, two), jnp.where(odd, two, one)
        return jnp.where(at > 0, before, 0.0), jnp.where(at < count - 1, behind, 0.0)

    across, along = me_ref[0] // lines, me_ref[0] & (lines - 1)
    up, down = sides(along, lines, along1_ref, along2_ref)
    left_side, right_side = sides(across, nparts, across1_ref, across2_ref)
    diffusion = diffusion_ref[...]
    first = iota((cols, width), 0) == 0
    last = iota((cols, width), 0) == cols - 1

    def row(i):
        if i < 0:
            return up
        if i >= rows_here:
            return down
        return mid_ref[pl.ds(i * cols, cols), :]

    stores = []
    above, here = row(-1), row(0)
    for i in range(rows_here):
        below = row(i + 1)
        if i == 0:
            left = pltpu.roll(here, 1, 0)
        else:
            left = mid_ref[pl.ds(i * cols - 1, cols), :]
        if i == rows_here - 1:
            right = pltpu.roll(here, cols - 1, 0)
        else:
            right = mid_ref[pl.ds(i * cols + 1, cols), :]
        left = jnp.where(first, left_side[i : i + 1, :], left)
        right = jnp.where(last, right_side[i : i + 1, :], right)
        courant = courant_ref[:, i : i + 1]
        out_ref[i] = (
            here
            - courant * (here - above)
            + diffusion * (above + below + left + right - 4.0 * here)
        )
        above, here = here, below
        if i % STEP == STEP - 1:
            piece = pl.ds(i + 1 - STEP, STEP)
            stores.append(
                pltpu.make_async_copy(out_ref.at[piece], out_hbm.at[piece], sems.at[i // STEP])
            )
            stores[-1].start()
    for store in stores:
        store.wait()


def transport(me, nparts, lines, reacted, halo, courant, diffusion):
    shape = (*courant.shape[::-1], reacted.shape[1])
    return pl.pallas_call(
        lambda *refs: transport_kernel(nparts, lines, *refs),
        out_shape=jax.ShapeDtypeStruct(shape, F32),
        in_specs=[pl.BlockSpec(memory_space=pltpu.SMEM)]
        + [pl.BlockSpec(memory_space=pltpu.VMEM)] * 7,
        out_specs=pl.BlockSpec(memory_space=pl.ANY),
        scratch_shapes=[
            pltpu.VMEM(shape, F32),
            pltpu.SemaphoreType.DMA((shape[0] // STEP,)),
        ],
        compiler_params=pltpu.CompilerParams(vmem_limit_bytes=20 << 20),
    )(me, reacted, *halo, courant, diffusion)


def swapped(block, axis, first):
    count = lax.axis_size(axis)
    pairs = [(i, (i + 1) % count) for i in range(first, count, 2)]
    return lax.ppermute(block, axis, pairs + [(j, i) for i, j in pairs])


def local(
    state, courant, diffusion, table_value, table_base, table_sens, slot_cell, hit_step, entry_ids
):
    rows_here, cols_here, width = state.shape
    cells = rows_here * cols_here
    nparts, lines = lax.axis_size("blk"), lax.axis_size("grid")
    me = lax.axis_index(("blk", "grid")).astype(jnp.int32).reshape(1)
    flat = state.reshape(cells, width)
    send, code, sens = pack(me, slot_cell[0], hit_step[0], flat, table_sens, nparts, lines)
    recv = lax.all_to_all(send.reshape(nparts, SEG, width), "blk", 0, 0, tiled=True)
    done = react(
        entry_ids, recv.reshape(nparts * SEG, width),
        table_value, table_base, sens, nparts,
    )
    back = lax.all_to_all(done.reshape(nparts, CAP, width), "blk", 0, 0, tiled=True)
    back = back.reshape(nparts * CAP, width)
    along1, along2, across1, across2 = edges(me, code, back, lines)
    halo = (
        swapped(along1, "grid", 0), swapped(along2, "grid", 1),
        swapped(across1, "blk", 0), swapped(across2, "blk", 1),
    )
    reacted = unpack(code, back)
    return transport(me, nparts, lines, reacted, halo, courant.T, diffusion.reshape(1, width))


def solution(mesh):
    return jax.shard_map(
        local,
        mesh=mesh,
        in_specs=(
            P("grid", "blk", None),
            P("grid", "blk"),
            P(),
            P("blk", None),
            P("blk", None),
            P("blk", None, None),
            P("grid", "blk", None),
            P("grid", "blk", None),
            P("blk", "grid", None),
        ),
        out_specs=P("grid", "blk", None),
        check_vma=False,
    )
```
